512 devices in a mesh: pool: 16 (over y, x_hi, core), batch: 32 (over z, x_lo).
Axes of the slice: x: 4 (x_hi: 2, x_lo: 2; x = x_hi * 2 + x_lo), y: 4, z: 16, core: 2. Of those that a mesh axis runs over, the one named last changes fastest.
Arguments:
- pooled_query_features: bfloat16 [65536, 768], P(('batch', 'pool'))
- item_features: bfloat16 [8192, 768], P(('pool', 'batch'))
- tower_weight: bfloat16 [768, 768], replicated, may hold values from -0.21875 to 0.21875
- item_counts: int32 [8192], P('pool'), may hold values from 1 to 4096
- positives: int32 [65536], P('batch'), may hold values from 0 to 8191
Outputs:
- mean_loss: float32 [], replicated
- weight_grad: float32 [768, 768], replicated
The draws below stay inside these ranges and needn't reach their ends.
All inputs are finite; a program needn't handle non-finite values.
Results may differ from the reference program's by a relative error of at most 0.015.
Values may be sent and summed in bfloat16 or wider, within the bound.
No kernel may reach another device: no remote copies, remote signals or barrier semaphores. Data moves between devices by JAX's collectives and lax.ppermute only.
A program may use at most 64 MiB of HBM per device.

```python
import jax
import jax.numpy as jnp
from jax import lax

D = 768
R_DEV = 128
I_DEV = 16
ROWS = 65536
ITEMS = 8192
N_POOL = 16
N_BATCH = 32


def common_tower_rows(key):
    return jax.random.normal(key, (ROWS, D), jnp.float32)


def draw_pooled_query_features(key, part):
    base = common_tower_rows(key)
    return base.astype(jnp.bfloat16)


def draw_item_features(key, part):
    key = jax.random.fold_in(key, 5)
    own = jax.random.normal(key, (ITEMS, D), jnp.float32)
    out = own
    return out.astype(jnp.bfloat16)


def with_ends(result, stream_key, smallest, high):
    extent = result.shape
    spot = [jax.random.randint(jax.random.fold_in(stream_key, axis), (), 0, extent[axis]) for axis in range(len(extent))]
    result = result.at[tuple(spot)].set(smallest)
    longest = extent.index(max(extent))
    spot[longest] = (spot[longest] + 1) % extent[longest]
    return result.at[tuple(spot)].set(high)


def normal_values(own_key, shape, spread, reach, held_as=jnp.bfloat16):
    return jnp.clip(spread * jax.random.normal(own_key, shape, jnp.float32), -reach, reach).astype(held_as)


def setup_inputs(seed: int = 0) -> dict:
    arg_keys = jax.random.split(jax.random.key(seed), 6)
    pooled_query_features = draw_pooled_query_features(jax.random.fold_in(arg_keys[5], 71), 0)
    item_features = draw_item_features(jax.random.fold_in(arg_keys[5], 71), 0)
    tower_weight = normal_values(arg_keys[2], (D, D), D ** -0.5, 0.21875)
    item_counts = with_ends(jax.random.randint(arg_keys[3], (ITEMS,), 1, 4097), jax.random.fold_in(arg_keys[3], 1), 1, 4096).astype(jnp.int32)
    positives = with_ends(jax.random.randint(arg_keys[4], (ROWS,), 0, ITEMS), jax.random.fold_in(arg_keys[4], 1), 0, ITEMS - 1).astype(jnp.int32)
    return dict(pooled_query_features=pooled_query_features, item_features=item_features, tower_weight=tower_weight, item_counts=item_counts, positives=positives)


def tower(feature_matrix, tower_weight):
    proj = jnp.dot(feature_matrix, tower_weight, preferred_element_type=jnp.float32)
    radius = jnp.sqrt(lax.optimization_barrier(jnp.sum(proj * proj, axis=1, keepdims=True)) + 1e-06)
    return (proj / radius, radius)

def back_norm(unit, radius, incoming_gradient):
    inner = lax.optimization_barrier(jnp.sum(unit * incoming_gradient, axis=1, keepdims=True))
    return (incoming_gradient - unit * inner) / radius

def reference(pooled_query_features, item_features, tower_weight, item_counts, positives):
    q_block = R_DEV * N_POOL
    i_block = I_DEV * N_BATCH
    eq, rq = tower(pooled_query_features, tower_weight)
    ei, ri = tower(item_features, tower_weight)
    eqb = eq.astype(jnp.bfloat16)
    eib = ei.astype(jnp.bfloat16)
    log_counts = jnp.log(item_counts.astype(jnp.float32))
    inv_norm = 1.0 / jnp.sqrt(jnp.float32(ROWS))
    item_cols = jnp.arange(ITEMS, dtype=jnp.int32)
    encoded_item_block_list = eib.astype(jnp.float32).reshape(N_POOL, i_block, -1)

    def per_block(carry, index):
        item_acc, loss_acc = carry
        start = (index * q_block).astype(jnp.int32)
        query_batch_rows = lax.dynamic_slice_in_dim(eqb, start, q_block, 0)
        targets = lax.dynamic_slice_in_dim(positives, start, q_block, 0)
        scores = 100.0 * jnp.dot(query_batch_rows, eib.T, preferred_element_type=jnp.float32) - log_counts[None, :]
        top = lax.optimization_barrier(jnp.max(scores, axis=1, keepdims=True))
        total = lax.optimization_barrier(jnp.sum(jnp.exp(scores - top), axis=1, keepdims=True))
        lse = top + jnp.log(total)
        hit = item_cols[None, :] == targets[:, None]
        pos_score = lax.optimization_barrier(jnp.sum(jnp.where(hit, scores, 0.0), axis=1))
        loss_acc = loss_acc + jnp.sum(lse[:, 0] - pos_score)
        grad = ((jnp.exp(scores - lse) - hit.astype(jnp.float32)) * inv_norm).astype(jnp.bfloat16)
        gradient_block_list = grad.astype(jnp.float32).reshape(q_block, N_POOL, i_block)
        partial_pieces = jnp.einsum('vse,seu->svu', gradient_block_list, encoded_item_block_list) * 100.0
        dq = lax.optimization_barrier(jnp.sum(partial_pieces.astype(jnp.bfloat16).astype(jnp.float32), axis=0))
        term = jnp.dot(grad.T, query_batch_rows, preferred_element_type=jnp.float32) * 100.0
        item_acc = item_acc + term.astype(jnp.bfloat16).astype(jnp.float32)
        return ((item_acc, loss_acc), dq)
    start_carry = (jnp.zeros((ITEMS, eq.shape[1]), jnp.float32), jnp.zeros((), jnp.float32))
    (di, loss_sum), dq_blocks = lax.scan(per_block, start_carry, jnp.arange(N_BATCH, dtype=jnp.int32))
    dq = dq_blocks.reshape(ROWS, -1)
    dzq = back_norm(eq, rq, dq)
    dzi = back_norm(ei, ri, di)
    highest = lax.Precision.HIGHEST
    weight_grad = jnp.dot(pooled_query_features.astype(jnp.float32).T, dzq, precision=highest)
    weight_grad = weight_grad + jnp.dot(item_features.astype(jnp.float32).T, dzi, precision=highest)
    return (loss_sum / jnp.float32(ROWS), weight_grad)
```

```python
import jax
import jax.numpy as jnp
from jax import lax
from jax.sharding import Mesh, PartitionSpec as P

BF = jnp.bfloat16
F32 = jnp.float32
D = 768
YX = ("y", "xh")
ROWS = 65536
INV_NORM = 1.0 / ROWS**0.5


def swap(x, axis):
    return lax.ppermute(x, axis, [(0, 1), (1, 0)])


def pair(x, axis):
    other = swap(x, axis)
    first = lax.axis_index(axis) == 0
    return jnp.stack([jnp.where(first, x, other), jnp.where(first, other, x)])


def exchange(x, axes):
    return lax.all_to_all(x, axes, 0, 0, tiled=True)


def gather(x, axes, n):
    return exchange(jnp.broadcast_to(x[None], (n,) + x.shape), axes)


def tower(features, weight):
    proj = jnp.dot(features, weight, preferred_element_type=F32)
    radius = jnp.sqrt(jnp.sum(proj * proj, axis=1, keepdims=True) + 1e-06)
    return (proj / radius).astype(BF), radius


def back_norm(unit, radius, incoming):
    unit = unit.astype(F32)
    inner = jnp.sum(unit * incoming, axis=1, keepdims=True)
    return ((incoming - unit * inner) / radius).astype(BF)


def dot(a, b, dims):
    return lax.dot_general(a, b, (dims, ((), ())), preferred_element_type=F32)


def split3(x):
    hi = x.astype(BF)
    mid = (x - hi.astype(F32)).astype(BF)
    low = (x - hi.astype(F32) - mid.astype(F32)).astype(BF)
    return jnp.stack([hi, mid, low])


def body(xq_own, xi_own, weight, counts, positives):
    core = lax.axis_index("c")
    xi = gather(pair(xi_own, "xl"), "z", 16).reshape(512, D)
    half = gather(xq_own, YX, 8).reshape(1024, D)
    xq = jnp.concatenate([half, swap(half, "c")], axis=0)
    targets = positives.reshape(8, 2, 128).transpose(1, 0, 2).reshape(2, 1024)
    targets = jnp.where(core == 0, targets, targets[::-1]).reshape(2048)

    eq, rq = tower(xq, weight)
    ei, ri = tower(xi, weight)
    scores = 100.0 * dot(eq, ei, ((1,), (1,))) - jnp.log(counts.astype(F32))[None, :]
    block = (lax.axis_index("y") * 2 + lax.axis_index("xh")) * 2 + core
    hit = (block * 512 + lax.iota(jnp.int32, 512))[None, :] == targets[:, None]
    top = jnp.max(scores, axis=1)
    lse = top + jnp.log(jnp.sum(jnp.exp(scores - top[:, None]), axis=1))
    pos = jnp.sum(jnp.where(hit, scores, 0.0))

    lse = lse.reshape(2, 1024)
    lse = jnp.where(core == 0, lse, lse[::-1])
    mine = jnp.concatenate([lse.reshape(16, 128), jnp.full((8, 128), pos, F32)])
    both = pair(mine, "c")
    lo = jnp.maximum(both[0, :16], both[1, :16])
    merged = lo + jnp.log(jnp.exp(both[0, :16] - lo) + jnp.exp(both[1, :16] - lo))
    merged = jnp.concatenate([merged, both[0, 16:] + both[1, 16:]])
    parts = gather(merged, YX, 8)
    tops = jnp.max(parts[:, :16], axis=0)
    lse = tops + jnp.log(jnp.sum(jnp.exp(parts[:, :16] - tops[None]), axis=0))
    loss = (jnp.sum(lse) - jnp.sum(parts[:, 16, 0])) / ROWS
    lse = lse.reshape(2, 1024)
    lse = jnp.where(core == 0, lse, lse[::-1]).reshape(2048)

    grad = ((jnp.exp(scores - lse[:, None]) - hit.astype(F32)) * INV_NORM).astype(BF)
    dzq = back_norm(eq, rq, 100.0 * dot(grad, ei, ((1,), (0,))))
    dzi = back_norm(ei, ri, 100.0 * dot(grad, eq, ((0,), (0,))))
    part = dot(xq, dzq, ((0,), (0,))) + dot(xi, dzi, ((0,), (0,)))

    part = part.astype(BF).reshape(2, 384, D)
    keep = jnp.where(core == 0, part[0], part[1])
    send = jnp.where(core == 0, part[1], part[0])
    s = (keep.astype(F32) + swap(send, "c").astype(F32)).astype(BF)
    s = jnp.sum(exchange(s.reshape(8, 48, D), YX).astype(F32), axis=0).astype(BF)
    s = s.reshape(32, 9, 128)
    tail = jnp.zeros((32, 1, 128), BF).at[:, 0, :3].set(split3(loss)[None])
    s = exchange(jnp.concatenate([s, tail], axis=1), ("z", "xl"))
    s = jnp.sum(s.astype(F32), axis=0)
    mean_loss = jnp.sum(s[9, :3])
    s = gather(s[:9].astype(BF), ("z", "xl"), 32).reshape(48, D)
    s = gather(s, YX, 8).reshape(384, D)
    return mean_loss, pair(s, "c").reshape(D, D).astype(F32)


def solution(mesh):
    fine = Mesh(mesh.devices.reshape(4, 2, 2, 16, 2), ("y", "xh", "c", "z", "xl"))
    pool, batch = ("y", "xh", "c"), ("z", "xl")
    return jax.shard_map(
        body,
        mesh=fine,
        in_specs=(P(batch + pool, None), P(pool + batch, None), P(), P(pool), P(batch)),
        out_specs=(P(), P()),
        check_vma=False,
    )
```

```python
import functools

import jax
import jax.numpy as jnp
from jax import lax
from jax.experimental import pallas as pl
from jax.experimental.pallas import tpu as pltpu
from jax.sharding import Mesh, PartitionSpec as P

BF = jnp.bfloat16
F32 = jnp.float32
D = 768
YX = ("y", "xh")
YXX = ("y", "xh", "xl")
POOL = ("y", "xh", "c")
ROWS = 65536
QB = 2048
IB = 512
HALF = 1024
CH = 512
INV_NORM = 1.0 / ROWS**0.5


def swap(x, axis):
    return lax.ppermute(x, axis, [(0, 1), (1, 0)])


def flip(x, k):
    return lax.ppermute(x, "z", [(i, i ^ k) for i in range(16)])


def exchange(x, axes):
    return lax.all_to_all(x, axes, 0, 0, tiled=True)


def gather(x, axes, n):
    return exchange(jnp.broadcast_to(x[None], (n,) + x.shape), axes)


def dot(a, b, dims):
    return lax.dot_general(a, b, (dims, ((), ())), preferred_element_type=F32)


def split3(x):
    hi = x.astype(BF)
    mid = (x - hi.astype(F32)).astype(BF)
    low = (x - hi.astype(F32) - mid.astype(F32)).astype(BF)
    return jnp.stack([hi, mid, low])


def unit_rows(x, weight):
    proj = dot(x, weight, ((1,), (0,)))
    inv = 1.0 / jnp.sqrt(jnp.sum(proj * proj, axis=1, keepdims=True) + 1e-06)
    return (proj * inv).astype(BF), inv


def tower_kernel(x_ref, w_ref, after_ref, e_ref, inv_ref):
    e_ref[...], inv_ref[...] = unit_rows(x_ref[...], w_ref[...])


def tower(x, weight, after, step):
    n = x.shape[0]
    return pl.pallas_call(
        tower_kernel,
        grid=(n // step,),
        in_specs=[
            pl.BlockSpec((step, D), lambda i: (i, 0)),
            pl.BlockSpec((D, D), lambda i: (0, 0)),
            pl.BlockSpec((16, 128), lambda i: (0, 0)),
        ],
        out_specs=[
            pl.BlockSpec((step, D), lambda i: (i, 0)),
            pl.BlockSpec((step, 1), lambda i: (i, 0)),
        ],
        out_shape=[jax.ShapeDtypeStruct((n, D), BF), jax.ShapeDtypeStruct((n, 1), F32)],
        compiler_params=pltpu.CompilerParams(vmem_limit_bytes=16 << 20),
        cost_estimate=pl.CostEstimate(flops=2 * n * D * D, bytes_accessed=4 * n * D, transcendentals=n),
        name="tower",
    )(x, weight, after)


def score_kernel(own_ref, other_ref, xi_ref, w_ref, logc_ref, ids_ref, tgt_ref,
                 ei_ref, invi_ref, exp_ref, top_ref, stat_ref):
    i = pl.program_id(0)

    @pl.when(i == 0)
    def _():
        ei_ref[...], invi_ref[...] = unit_rows(xi_ref[...], w_ref[...])
        stat_ref[2] = jnp.zeros_like(stat_ref[2])

    def run(eq):
        scores = 100.0 * dot(ei_ref[...], eq, ((1,), (1,))) - logc_ref[...]
        top = jnp.max(scores, axis=0, keepdims=True)
        e = jnp.exp(scores - top)
        exp_ref[...] = e
        top_ref[...] = top
        lse = top + jnp.log(jnp.sum(e, axis=0, keepdims=True))
        hit = ids_ref[...] == tgt_ref[...]
        pos = jnp.sum(jnp.where(hit, scores, 0.0), axis=0, keepdims=True)
        lanes = pl.ds(pl.multiple_of((i % 2) * CH, CH), CH)
        stat_ref[i // 2, :, lanes] = lse
        stat_ref[2, :, lanes] = stat_ref[2, :, lanes] + pos

    @pl.when(i < 2)
    def _():
        run(own_ref[...])

    @pl.when(i >= 2)
    def _():
        run(other_ref[...])


def score(own, other, xi, weight, logc, ids, targets):
    whole = lambda *s: pl.BlockSpec(s, lambda i: (0,) * len(s))
    return pl.pallas_call(
        score_kernel,
        grid=(QB // CH,),
        in_specs=[
            pl.BlockSpec((CH, D), lambda i: (jnp.minimum(i, 1), 0)),
            pl.BlockSpec((CH, D), lambda i: (jnp.maximum(i - 2, 0), 0)),
            whole(IB, D),
            whole(D, D),
            whole(IB, 1),
            whole(IB, 1),
            pl.BlockSpec((1, CH), lambda i: (0, i)),
        ],
        out_specs=[
            whole(IB, D),
            whole(IB, 1),
            pl.BlockSpec((IB, CH), lambda i: (0, i)),
            pl.BlockSpec((1, CH), lambda i: (0, i)),
            whole(3, 1, HALF),
        ],
        out_shape=[
            jax.ShapeDtypeStruct((IB, D), BF),
            jax.ShapeDtypeStruct((IB, 1), F32),
            jax.ShapeDtypeStruct((IB, QB), F32),
            jax.ShapeDtypeStruct((1, QB), F32),
            jax.ShapeDtypeStruct((3, 1, HALF), F32),
        ],
        compiler_params=pltpu.CompilerParams(vmem_limit_bytes=24 << 20),
        cost_estimate=pl.CostEstimate(
            flops=2 * IB * D * (D + QB), bytes_accessed=10 << 20, transcendentals=IB * QB
        ),
        name="score",
    )(own, other, xi, weight, logc, ids, targets)


def grad_kernel(core_ref, parts_ref, exp_ref, top_ref, eqa_ref, eqb_ref, inva_ref, invb_ref, xqa_ref, xqb_ref,
                ei_ref, invi_ref, xi_ref, ids_ref, tgt_ref,
                send_ref, keep_ref, loss_ref, lse_ref, di_ref, acc_ref):
    i = pl.program_id(0)
    core = core_ref[0]

    @pl.when(i == 0)
    def _():
        total = jnp.zeros((1, HALF), F32)
        for h in range(2):
            vals = []
            for d in range(8):
                vals.append(parts_ref[2 * d + core, h])
                vals.append(parts_ref[2 * d + 1 - core, 1 - h])
            top = functools.reduce(jnp.maximum, vals)
            lse = top + jnp.log(sum(jnp.exp(v - top) for v in vals))
            lse_ref[h] = lse
            total = total + lse
        for d in range(16):
            total = total - parts_ref[d, 2]
        loss_ref[...] = jnp.broadcast_to(jnp.sum(total, axis=1, keepdims=True), (8, 128))
        di_ref[...] = jnp.zeros_like(di_ref)
        acc_ref[...] = jnp.zeros_like(acc_ref)

    def run(eq_ref, inv_ref, xq_ref):
        lanes = pl.ds(pl.multiple_of((i % 2) * CH, CH), CH)
        scale = jnp.exp(top_ref[...] - lse_ref[i // 2, :, lanes])
        hit = ids_ref[...] == tgt_ref[...]
        grad = ((exp_ref[...] * scale - jnp.where(hit, 1.0, 0.0)) * INV_NORM).astype(BF)
        eq = eq_ref[...]
        di_ref[...] += dot(grad, eq, ((1,), (0,)))
        dq = 100.0 * dot(grad, ei_ref[...], ((0,), (0,)))
        eq = eq.astype(F32)
        inner = jnp.sum(eq * dq, axis=1, keepdims=True)
        dz = ((dq - eq * inner) * inv_ref[...]).astype(BF)
        acc_ref[...] += dot(xq_ref[...], dz, ((0,), (0,)))

    @pl.when(i < 2)
    def _():
        run(eqa_ref, inva_ref, xqa_ref)

    @pl.when(i >= 2)
    def _():
        run(eqb_ref, invb_ref, xqb_ref)

    @pl.when(i == QB // CH - 1)
    def _():
        di = 100.0 * di_ref[...]
        ei = ei_ref[...].astype(F32)
        inner = jnp.sum(ei * di, axis=1, keepdims=True)
        dz = ((di - ei * inner) * invi_ref[...]).astype(BF)
        acc_ref[...] += dot(xi_ref[...], dz, ((0,), (0,)))
        mine = pl.ds(pl.multiple_of(core * (D // 2), D // 2), D // 2)
        theirs = pl.ds(pl.multiple_of((1 - core) * (D // 2), D // 2), D // 2)
        keep_ref[...] = acc_ref[mine, :].astype(BF)
        send_ref[...] = acc_ref[theirs, :].astype(BF)


def grads(core, parts, e, top, eqa, eqb, inva, invb, xqa, xqb, ei, invi, xi, ids, targets):
    whole = lambda *s: pl.BlockSpec(s, lambda i: (0,) * len(s))
    first = lambda c: pl.BlockSpec((CH, c), lambda i: (jnp.minimum(i, 1), 0))
    second = lambda c: pl.BlockSpec((CH, c), lambda i: (jnp.maximum(i - 2, 0), 0))
    return pl.pallas_call(
        grad_kernel,
        grid=(QB // CH,),
        in_specs=[
            pl.BlockSpec(memory_space=pltpu.SMEM),
            whole(16, 3, 1, HALF),
            pl.BlockSpec((IB, CH), lambda i: (0, i)),
            pl.BlockSpec((1, CH), lambda i: (0, i)),
            first(D),
            second(D),
            first(1),
            second(1),
            first(D),
            second(D),
            whole(IB, D),
            whole(IB, 1),
            whole(IB, D),
            whole(IB, 1),
            pl.BlockSpec((1, CH), lambda i: (0, i)),
        ],
        out_specs=[whole(D // 2, D), whole(D // 2, D), whole(8, 128)],
        out_shape=[
            jax.ShapeDtypeStruct((D // 2, D), BF),
            jax.ShapeDtypeStruct((D // 2, D), BF),
            jax.ShapeDtypeStruct((8, 128), F32),
        ],
        scratch_shapes=[
            pltpu.VMEM((2, 1, HALF), F32),
            pltpu.VMEM((IB, D), F32),
            pltpu.VMEM((D, D), F32),
        ],
        compiler_params=pltpu.CompilerParams(vmem_limit_bytes=32 << 20),
        cost_estimate=pl.CostEstimate(
            flops=2 * IB * D * 2 * QB + 2 * D * D * (QB + IB), bytes_accessed=14 << 20, transcendentals=QB
        ),
        name="grads",
    )(core, parts, e, top, eqa, eqb, inva, invb, xqa, xqb, ei, invi, xi, ids, targets)


def body(xq_own, xi_own, weight, counts, positives):
    core = lax.axis_index("c")
    z, xl = lax.axis_index("z"), lax.axis_index("xl")
    xqa = gather(xq_own, YX, 8).reshape(HALF, D)
    xi = xi_own
    for k in (8, 4, 2, 1):
        xi = jnp.concatenate([xi, flip(xi, k)])
    near = xi
    xi = jnp.concatenate([xi, swap(xi, "xl")])

    at = lax.iota(jnp.int32, IB)
    p = (at // 16) % 16
    bits = (p % 2) * 8 + (p // 2 % 2) * 4 + (p // 4 % 2) * 2 + p // 8
    ids = ((z ^ bits) * 2 + (xl ^ (at // 256))) * 16 + at % 16
    logs = jnp.log(counts.astype(F32))
    logc = jnp.sum(jnp.where(ids[:, None] == at[None, :], logs[None, :], 0.0), axis=1, keepdims=True)
    block = (lax.axis_index("y") * 2 + lax.axis_index("xh")) * 2 + core
    ids = (block * IB + ids)[:, None]
    targets = positives.reshape(8, 2, 128).transpose(1, 0, 2)
    targets = jnp.where(core == 0, targets, jnp.concatenate([targets[1:], targets[:1]])).reshape(1, QB)

    eqa, inva = tower(xqa, weight, near, 512)
    eqb, invb = swap(eqa, "c"), swap(inva, "c")
    xqb = swap(xqa, "c")
    ei, invi, e, top, stat = score(eqa, eqb, xi, weight, logc, ids, targets)
    parts = gather(stat, POOL, 16)
    send, keep, loss = grads(
        core.reshape(1), parts, e, top, eqa, eqb, inva, invb, xqa, xqb, ei, invi, xi, ids, targets
    )

    loss = (loss + swap(loss, "xl"))[0, 0] / ROWS
    s = (keep.astype(F32) + swap(send, "c").astype(F32)).astype(BF)
    s = jnp.sum(exchange(s.reshape(16, 24, D), YXX).astype(F32), axis=0).astype(BF)
    s = s.reshape(16, 9, 128)
    tail = jnp.zeros((16, 1, 128), BF).at[:, 0, :3].set(split3(loss)[None])
    s = exchange(jnp.concatenate([s, tail], axis=1), "z")
    s = jnp.sum(s.astype(F32), axis=0)
    mean_loss = jnp.sum(s[9, :3])
    s = gather(s[:9].astype(BF), "z", 16).reshape(24, D)
    s = gather(s, YXX, 16).reshape(D // 2, D)
    other = swap(s, "c")
    first, second = jnp.where(core == 0, s, other), jnp.where(core == 0, other, s)
    return mean_loss, jnp.concatenate([first, second]).astype(F32)


def solution(mesh):
    fine = Mesh(mesh.devices.reshape(4, 2, 2, 16, 2), ("y", "xh", "c", "z", "xl"))
    batch = ("z", "xl")
    return jax.shard_map(
        body,
        mesh=fine,
        in_specs=(P(batch + POOL, None), P(POOL + batch, None), P(), P(POOL), P(batch)),
        out_specs=(P(), P()),
        check_vma=False,
    )
```

```python
import functools

import jax
import jax.numpy as jnp
from jax import lax
from jax.experimental import pallas as pl
from jax.experimental.pallas import tpu as pltpu
from jax.sharding import Mesh, PartitionSpec as P

BF = jnp.bfloat16
F32 = jnp.float32
D = 768
YX = ("y", "xh")
YXX = ("y", "xh", "xl")
POOL = ("y", "xh", "c")
ROWS = 65536
QB = 2048
IB = 512
HALF = 1024
CH = 512
INV_NORM = 1.0 / ROWS**0.5


def swap(x, axis):
    return lax.ppermute(x, axis, [(0, 1), (1, 0)])


def turn(x, k):
    return lax.ppermute(x, "y", [(i, (i + k) % 4) for i in range(4)])


def exchange(x, axes):
    return lax.all_to_all(x, axes, 0, 0, tiled=True)


def gather(x, axes, n):
    return exchange(jnp.broadcast_to(x[None], (n,) + x.shape), axes)


def dot(a, b, dims):
    return lax.dot_general(a, b, (dims, ((), ())), preferred_element_type=F32)


def split3(x):
    hi = x.astype(BF)
    mid = (x - hi.astype(F32)).astype(BF)
    low = (x - hi.astype(F32) - mid.astype(F32)).astype(BF)
    return jnp.stack([hi, mid, low])


def unit_rows(x, weight):
    proj = dot(x, weight, ((1,), (0,)))
    inv = 1.0 / jnp.sqrt(jnp.sum(proj * proj, axis=1, keepdims=True) + 1e-06)
    return (proj * inv).astype(BF), inv


def score_tile(ei_ref, eq, logc_ref):
    return 100.0 * dot(ei_ref[...], eq, ((1,), (1,))) - logc_ref[...]


def whole(*s):
    return pl.BlockSpec(s, lambda i: (0,) * len(s))


def first(c):
    return pl.BlockSpec((CH, c), lambda i: (jnp.minimum(i, HALF // CH - 1), 0))


def second(c):
    return pl.BlockSpec((CH, c), lambda i: (jnp.maximum(i - HALF // CH, 0), 0))


def copies_kernel(xl_ref, mine_ref, other_ref, after_ref, out_ref):
    xl = xl_ref[0]
    out_ref[0, xl] = mine_ref[...]
    out_ref[0, 1 - xl] = other_ref[...]


def copies(xl, mine, other, after):
    n = mine.shape[0]
    return pl.pallas_call(
        copies_kernel,
        grid=(16,),
        in_specs=[
            pl.BlockSpec(memory_space=pltpu.SMEM),
            whole(n, D),
            whole(n, D),
            pl.BlockSpec(memory_space=pl.ANY),
        ],
        out_specs=pl.BlockSpec((1, 2, n, D), lambda i: (i, 0, 0, 0)),
        out_shape=jax.ShapeDtypeStruct((16, 2, n, D), BF),
        compiler_params=pltpu.CompilerParams(vmem_limit_bytes=4 << 20),
        cost_estimate=pl.CostEstimate(flops=0, bytes_accessed=32 * n * D * 2, transcendentals=0),
        name="copies",
    )(xl.reshape(1), mine, other, after)


def tower_kernel(x_ref, w_ref, e_ref, inv_ref):
    e_ref[...], inv_ref[...] = unit_rows(x_ref[...], w_ref[...])


def tower(x, weight):
    return pl.pallas_call(
        tower_kernel,
        grid=(HALF // CH,),
        in_specs=[pl.BlockSpec((CH, D), lambda i: (i, 0)), whole(D, D)],
        out_specs=[pl.BlockSpec((CH, D), lambda i: (i, 0)), pl.BlockSpec((CH, 1), lambda i: (i, 0))],
        out_shape=[pltpu.HBM((HALF, D), BF), pltpu.HBM((HALF, 1), F32)],
        compiler_params=pltpu.CompilerParams(vmem_limit_bytes=16 << 20),
        cost_estimate=pl.CostEstimate(flops=2 * HALF * D * D, bytes_accessed=4 * HALF * D, transcendentals=HALF),
        name="tower",
    )(x, weight)


def score_kernel(order_ref, eqa_ref, eqb_ref, w_ref, xi_ref, logc_ref, ids_ref, tgt_ref,
                 ei_ref, invi_ref, stat_ref):
    i = pl.program_id(0)

    @pl.when(i == 0)
    def _():
        ei_ref[...], invi_ref[...] = unit_rows(xi_ref[...], w_ref[...])
        stat_ref[...] = jnp.zeros_like(stat_ref)

    def run(eq):
        scores = score_tile(ei_ref, eq, logc_ref)
        top = jnp.max(scores, axis=0, keepdims=True)
        lse = top + jnp.log(jnp.sum(jnp.exp(scores - top), axis=0, keepdims=True))
        pos = jnp.sum(jnp.where(ids_ref[...] == tgt_ref[...], scores, 0.0), axis=0, keepdims=True)
        for k in range(CH // 128):
            part = slice(k * 128, (k + 1) * 128)
            stat_ref[pl.ds(order_ref[i * (CH // 128) + k], 1), :] = lse[:, part]
            stat_ref[16:17, :] = stat_ref[16:17, :] + pos[:, part]

    @pl.when(i < HALF // CH)
    def _():
        run(eqa_ref[...])

    @pl.when(i >= HALF // CH)
    def _():
        run(eqb_ref[...])


def score(order, eqa, eqb, weight, xi, logc, ids, targets):
    return pl.pallas_call(
        score_kernel,
        grid=(QB // CH,),
        in_specs=[
            pl.BlockSpec(memory_space=pltpu.SMEM),
            first(D),
            second(D),
            whole(D, D),
            whole(IB, D),
            whole(IB, 1),
            whole(IB, 1),
            pl.BlockSpec((1, CH), lambda i: (0, i)),
        ],
        out_specs=[whole(IB, D), whole(IB, 1), whole(24, 128)],
        out_shape=[
            jax.ShapeDtypeStruct((IB, D), BF),
            jax.ShapeDtypeStruct((IB, 1), F32),
            jax.ShapeDtypeStruct((24, 128), F32),
        ],
        compiler_params=pltpu.CompilerParams(vmem_limit_bytes=24 << 20),
        cost_estimate=pl.CostEstimate(
            flops=2 * IB * D * (D + QB), bytes_accessed=6 << 20, transcendentals=IB * QB
        ),
        name="score",
    )(order, eqa, eqb, weight, xi, logc, ids, targets)


def grad_kernel(core_ref, order_ref, parts_ref, eqa_ref, eqb_ref, inva_ref, invb_ref, xqa_ref, xqb_ref,
                ei_ref, invi_ref, xi_ref, logc_ref, ids_ref, tgt_ref,
                send_ref, keep_ref, loss_ref, lse_ref, di_ref, acc_ref):
    i = pl.program_id(0)
    core = core_ref[0]

    @pl.when(i == 0)
    def _():
        vals = [parts_ref[d, :16, :] for d in range(16)]
        top = functools.reduce(jnp.maximum, vals)
        lse = top + jnp.log(sum(jnp.exp(v - top) for v in vals))
        lse_ref[...] = lse
        pos = sum(parts_ref[d, 16:17, :] for d in range(16))
        total = jnp.sum(jnp.sum(lse, axis=0, keepdims=True) - pos, axis=1, keepdims=True)
        loss_ref[...] = jnp.broadcast_to(total, (8, 128))
        di_ref[...] = jnp.zeros_like(di_ref)
        acc_ref[...] = jnp.zeros_like(acc_ref)

    def run(eq_ref, inv_ref, xq_ref):
        eq = eq_ref[...]
        rows = [order_ref[i * (CH // 128) + k] for k in range(CH // 128)]
        lse = jnp.concatenate([lse_ref[pl.ds(r, 1), :] for r in rows], axis=1)
        prob = jnp.exp(score_tile(ei_ref, eq, logc_ref) - lse)
        hit = ids_ref[...] == tgt_ref[...]
        grad = ((prob - jnp.where(hit, 1.0, 0.0)) * INV_NORM).astype(BF)
        di_ref[...] += dot(grad, eq, ((1,), (0,)))
        dq = 100.0 * dot(grad, ei_ref[...], ((0,), (0,)))
        eq = eq.astype(F32)
        inner = jnp.sum(eq * dq, axis=1, keepdims=True)
        dz = ((dq - eq * inner) * inv_ref[...]).astype(BF)
        acc_ref[...] += dot(xq_ref[...], dz, ((0,), (0,)))

    @pl.when(i < HALF // CH)
    def _():
        run(eqa_ref, inva_ref, xqa_ref)

    @pl.when(i >= HALF // CH)
    def _():
        run(eqb_ref, invb_ref, xqb_ref)

    @pl.when(i == QB // CH - 1)
    def _():
        di = 100.0 * di_ref[...]
        ei = ei_ref[...].astype(F32)
        inner = jnp.sum(ei * di, axis=1, keepdims=True)
        dz = ((di - ei * inner) * invi_ref[...]).astype(BF)
        acc_ref[...] += dot(xi_ref[...], dz, ((0,), (0,)))
        mine = pl.ds(pl.multiple_of(core * (D // 2), D // 2), D // 2)
        theirs = pl.ds(pl.multiple_of((1 - core) * (D // 2), D // 2), D // 2)
        keep_ref[...] = acc_ref[mine, :].astype(BF)
        send_ref[...] = acc_ref[theirs, :].astype(BF)


def grads(core, order, parts, eqa, eqb, inva, invb, xqa, xqb, ei, invi, xi, logc, ids, targets):
    return pl.pallas_call(
        grad_kernel,
        grid=(QB // CH,),
        in_specs=[
            pl.BlockSpec(memory_space=pltpu.SMEM),
            pl.BlockSpec(memory_space=pltpu.SMEM),
            whole(16, 24, 128),
            first(D),
            second(D),
            first(1),
            second(1),
            first(D),
            second(D),
            whole(IB, D),
            whole(IB, 1),
            whole(IB, D),
            whole(IB, 1),
            whole(IB, 1),
            pl.BlockSpec((1, CH), lambda i: (0, i)),
        ],
        out_specs=[whole(D // 2, D), whole(D // 2, D), whole(8, 128)],
        out_shape=[
            jax.ShapeDtypeStruct((D // 2, D), BF),
            jax.ShapeDtypeStruct((D // 2, D), BF),
            jax.ShapeDtypeStruct((8, 128), F32),
        ],
        scratch_shapes=[
            pltpu.VMEM((16, 128), F32),
            pltpu.VMEM((IB, D), F32),
            pltpu.VMEM((D, D), F32),
        ],
        compiler_params=pltpu.CompilerParams(vmem_limit_bytes=32 << 20),
        cost_estimate=pl.CostEstimate(
            flops=2 * IB * D * 3 * QB + 2 * D * D * (QB + IB), bytes_accessed=9 << 20, transcendentals=IB * QB
        ),
        name="grads",
    )(core, order, parts, eqa, eqb, inva, invb, xqa, xqb, ei, invi, xi, logc, ids, targets)


def body(xq_own, xi_own, weight, counts, positives):
    core, y, xh = lax.axis_index("c"), lax.axis_index("y"), lax.axis_index("xh")
    xl = lax.axis_index("xl")
    far = swap(xi_own, "xl")
    side = swap(xq_own, "xh")
    two = jnp.concatenate([xq_own, side])
    xqa = jnp.concatenate([two, turn(two, 1), turn(two, 3), turn(two, 2)])
    xqb = swap(xqa, "c")
    xi = exchange(copies(xl, xi_own, far, side), "z").reshape(IB, D)

    q = lax.iota(jnp.int32, 16)
    step = (q // 2) % 4
    from_y = (y + jnp.where(step == 1, 3, jnp.where(step == 2, 1, jnp.where(step == 3, 2, 0)))) % 4
    order = from_y * 4 + (xh ^ (q % 2)) * 2 + (core ^ (q // 8))
    picks = order[:, None, None] == q[None, :, None]
    targets = jnp.sum(jnp.where(picks, positives.reshape(1, 16, 128), 0), axis=1).reshape(1, QB)
    block = (y * 2 + xh) * 2 + core
    ids = (block * IB + lax.iota(jnp.int32, IB))[:, None]
    logc = jnp.log(counts.astype(F32))[:, None]

    eqa, inva = tower(xqa, weight)
    eqb, invb = tower(xqb, weight)
    ei, invi, stat = score(order, eqa, eqb, weight, xi, logc, ids, targets)
    parts = gather(stat, POOL, 16)
    send, keep, loss = grads(
        core.reshape(1), order, parts, eqa, eqb, inva, invb, xqa, xqb, ei, invi, xi, logc, ids, targets
    )

    loss = (loss + swap(loss, "xl"))[0, 0] / ROWS
    s = (keep.astype(F32) + swap(send, "c").astype(F32)).astype(BF)
    s = jnp.sum(exchange(s.reshape(16, 24, D), YXX).astype(F32), axis=0).astype(BF)
    tail = jnp.zeros((7, 128), BF).at[0, :3].set(split3(loss))
    tail = jnp.broadcast_to(tail[None], (16, 7, 128))
    s = exchange(jnp.concatenate([s.reshape(16, 9, 128), tail], axis=1), "z")
    s = jnp.sum(s.astype(F32), axis=0)
    mean_loss = jnp.sum(s[9, :3])
    s = gather(s.astype(BF), "z", 16)[:, :9]
    s = gather(s.reshape(24, D), YXX, 16).reshape(D // 2, D)
    other = swap(s, "c")
    first, second = jnp.where(core == 0, s, other), jnp.where(core == 0, other, s)
    return mean_loss, jnp.concatenate([first, second]).astype(F32)


def solution(mesh):
    fine = Mesh(mesh.devices.reshape(4, 2, 2, 16, 2), ("y", "xh", "c", "z", "xl"))
    batch = ("z", "xl")
    return jax.shard_map(
        body,
        mesh=fine,
        in_specs=(P(batch + POOL, None), P(POOL + batch, None), P(), P(POOL), P(batch)),
        out_specs=(P(), P()),
        check_vma=False,
    )
```

```python
import functools

import jax
import jax.numpy as jnp
from jax import lax
from jax.experimental import pallas as pl
from jax.experimental.pallas import tpu as pltpu
from jax.sharding import Mesh, PartitionSpec as P

BF = jnp.bfloat16
F32 = jnp.float32
D = 768
YX = ("y", "xh")
YXX = ("y", "xh", "xl")
POOL = ("y", "xh", "c")
ROWS = 65536
QB = 2048
IB = 512
HALF = 1024
CH = 512
CG = 512
INV_NORM = 1.0 / ROWS**0.5
LOG2_NORM = -8.0
LOG2E = 1.4426950408889634


def swap(x, axis):
    return lax.ppermute(x, axis, [(0, 1), (1, 0)])


def turn(x, k):
    return lax.ppermute(x, "y", [(i, (i + k) % 4) for i in range(4)])


def exchange(x, axes):
    return lax.all_to_all(x, axes, 0, 0, tiled=True)


def gather(x, axes, n):
    return exchange(jnp.broadcast_to(x[None], (n,) + x.shape), axes)


def dot(a, b, dims):
    return lax.dot_general(a, b, (dims, ((), ())), preferred_element_type=F32)


def split3(x):
    hi = x.astype(BF)
    mid = (x - hi.astype(F32)).astype(BF)
    low = (x - hi.astype(F32) - mid.astype(F32)).astype(BF)
    return jnp.stack([hi, mid, low])


def unit_rows(x, weight):
    proj = dot(x, weight, ((1,), (0,)))
    inv = 1.0 / jnp.sqrt(jnp.sum(proj * proj, axis=1, keepdims=True) + 1e-06)
    return (proj * inv).astype(BF), inv


def score_tile(ei_ref, eq, logc_ref):
    return 100.0 * dot(ei_ref[...], eq, ((1,), (1,))) - logc_ref[...]


def whole(*s):
    return pl.BlockSpec(s, lambda i: (0,) * len(s))


def first(n, c):
    return pl.BlockSpec((n, c), lambda i: (jnp.minimum(i, HALF // n - 1), 0))


def second(n, c):
    return pl.BlockSpec((n, c), lambda i: (jnp.maximum(i - HALF // n, 0), 0))


def join_kernel(two_ref, a_ref, b_ref, c_ref, after_ref, out_ref):
    n = two_ref.shape[0]
    for k, ref in enumerate((two_ref, a_ref, b_ref, c_ref)):
        out_ref[k * n:(k + 1) * n, :] = ref[...]


def join(two, a, b, c, after):
    n = two.shape[0]
    return pl.pallas_call(
        join_kernel,
        in_specs=[pl.BlockSpec(memory_space=pltpu.VMEM)] * 4 + [pl.BlockSpec(memory_space=pl.ANY)],
        out_specs=pl.BlockSpec(memory_space=pltpu.VMEM),
        out_shape=jax.ShapeDtypeStruct((4 * n, D), BF),
        compiler_params=pltpu.CompilerParams(vmem_limit_bytes=8 << 20),
        cost_estimate=pl.CostEstimate(flops=0, bytes_accessed=16 * n * D, transcendentals=0),
        name="join",
    )(two, a, b, c, after)


def tower_kernel(x_ref, w_ref, e_ref, inv_ref):
    e_ref[...], inv_ref[...] = unit_rows(x_ref[...], w_ref[...])


def tower(x, weight):
    return pl.pallas_call(
        tower_kernel,
        grid=(HALF // CH,),
        in_specs=[pl.BlockSpec((CH, D), lambda i: (i, 0)), whole(D, D)],
        out_specs=[pl.BlockSpec((CH, D), lambda i: (i, 0)), pl.BlockSpec((CH, 1), lambda i: (i, 0))],
        out_shape=[pltpu.HBM((HALF, D), BF), pltpu.HBM((HALF, 1), F32)],
        compiler_params=pltpu.CompilerParams(vmem_limit_bytes=16 << 20),
        cost_estimate=pl.CostEstimate(flops=2 * HALF * D * D, bytes_accessed=4 * HALF * D, transcendentals=HALF),
        name="tower",
    )(x, weight)


def score_kernel(order_ref, eqa_ref, eqb_ref, w_ref, near_ref, far_ref, logc_ref, ids_ref, tgt_ref,
                 ei_ref, invi_ref, stat_ref):
    i = pl.program_id(0)

    @pl.when(i == 0)
    def _():
        for k, ref in enumerate((near_ref, far_ref)):
            part = slice(k * (IB // 2), (k + 1) * (IB // 2))
            ei_ref[part, :], invi_ref[part, :] = unit_rows(ref[...], w_ref[...])
        stat_ref[...] = jnp.zeros_like(stat_ref)

    def run(eq):
        scores = score_tile(ei_ref, eq, logc_ref)
        top = jnp.max(scores, axis=0, keepdims=True)
        lse = top + jnp.log(jnp.sum(jnp.exp(scores - top), axis=0, keepdims=True))
        pos = jnp.sum(jnp.where(ids_ref[...] == tgt_ref[...], scores, 0.0), axis=0, keepdims=True)
        for k in range(CH // 128):
            part = slice(k * 128, (k + 1) * 128)
            stat_ref[pl.ds(order_ref[i * (CH // 128) + k], 1), :] = lse[:, part]
            stat_ref[16:17, :] = stat_ref[16:17, :] + pos[:, part]

    @pl.when(i < HALF // CH)
    def _():
        run(eqa_ref[...])

    @pl.when(i >= HALF // CH)
    def _():
        run(eqb_ref[...])


def score(order, eqa, eqb, weight, near, far, logc, ids, targets):
    return pl.pallas_call(
        score_kernel,
        grid=(QB // CH,),
        in_specs=[
            pl.BlockSpec(memory_space=pltpu.SMEM),
            first(CH, D),
            second(CH, D),
            whole(D, D),
            whole(IB // 2, D),
            whole(IB // 2, D),
            whole(IB, 1),
            whole(IB, 1),
            pl.BlockSpec((1, CH), lambda i: (0, i)),
        ],
        out_specs=[whole(IB, D), whole(IB, 1), whole(24, 128)],
        out_shape=[
            jax.ShapeDtypeStruct((IB, D), BF),
            jax.ShapeDtypeStruct((IB, 1), F32),
            jax.ShapeDtypeStruct((24, 128), F32),
        ],
        compiler_params=pltpu.CompilerParams(vmem_limit_bytes=24 << 20),
        cost_estimate=pl.CostEstimate(
            flops=2 * IB * D * (D + QB), bytes_accessed=6 << 20, transcendentals=IB * QB
        ),
        name="score",
    )(order, eqa, eqb, weight, near, far, logc, ids, targets)


def grad_kernel(core_ref, order_ref, parts_ref, eqa_ref, eqb_ref, inva_ref, invb_ref, xqa_ref, xqb_ref,
                ei_ref, invi_ref, near_ref, far_ref, logc_ref, ids_ref, tgt_ref,
                send_ref, keep_ref, loss_ref, lse_ref, di_ref, acc_ref):
    i = pl.program_id(0)
    core = core_ref[0]

    @pl.when(i == 0)
    def _():
        vals = [parts_ref[d, :16, :] for d in range(16)]
        top = functools.reduce(jnp.maximum, vals)
        lse = top + jnp.log(sum(jnp.exp(v - top) for v in vals))
        lse_ref[...] = lse
        pos = sum(parts_ref[d, 16:17, :] for d in range(16))
        total = jnp.sum(jnp.sum(lse, axis=0, keepdims=True) - pos, axis=1, keepdims=True)
        loss_ref[...] = jnp.broadcast_to(total, (8, 128))
        di_ref[...] = jnp.zeros_like(di_ref)
        acc_ref[...] = jnp.zeros_like(acc_ref)

    def run(eq_ref, inv_ref, xq_ref):
        eq = eq_ref[...]
        rows = [order_ref[i * (CG // 128) + k] for k in range(CG // 128)]
        lse = jnp.concatenate([lse_ref[pl.ds(r, 1), :] for r in rows], axis=1)
        power = dot(ei_ref[...], eq, ((1,), (1,))) * (100.0 * LOG2E) - logc_ref[...] * LOG2E
        prob = jnp.exp2(power - (lse * LOG2E - LOG2_NORM))
        grad = jnp.where(ids_ref[...] == tgt_ref[...], prob - INV_NORM, prob).astype(BF)
        di_ref[...] += dot(grad, eq, ((1,), (0,)))
        dq = dot(grad, ei_ref[...], ((0,), (0,)))
        eq = eq.astype(F32)
        inner = jnp.sum(eq * dq, axis=1, keepdims=True)
        dz = ((dq - eq * inner) * (100.0 * inv_ref[...])).astype(BF)
        acc_ref[...] += dot(xq_ref[...], dz, ((0,), (0,)))

    @pl.when(i < HALF // CG)
    def _():
        run(eqa_ref, inva_ref, xqa_ref)

    @pl.when(i >= HALF // CG)
    def _():
        run(eqb_ref, invb_ref, xqb_ref)

    @pl.when(i == QB // CG - 1)
    def _():
        di = 100.0 * di_ref[...]
        ei = ei_ref[...].astype(F32)
        inner = jnp.sum(ei * di, axis=1, keepdims=True)
        dz = ((di - ei * inner) * invi_ref[...]).astype(BF)
        for k, ref in enumerate((near_ref, far_ref)):
            acc_ref[...] += dot(ref[...], dz[k * (IB // 2):(k + 1) * (IB // 2)], ((0,), (0,)))
        mine = pl.ds(pl.multiple_of(core * (D // 2), D // 2), D // 2)
        theirs = pl.ds(pl.multiple_of((1 - core) * (D // 2), D // 2), D // 2)
        keep_ref[...] = acc_ref[mine, :].astype(BF)
        send_ref[...] = acc_ref[theirs, :].astype(BF)


def grads(core, order, parts, eqa, eqb, inva, invb, xqa, xqb, ei, invi, near, far, logc, ids, targets):
    return pl.pallas_call(
        grad_kernel,
        grid=(QB // CG,),
        in_specs=[
            pl.BlockSpec(memory_space=pltpu.SMEM),
            pl.BlockSpec(memory_space=pltpu.SMEM),
            whole(16, 24, 128),
            first(CG, D),
            second(CG, D),
            first(CG, 1),
            second(CG, 1),
            first(CG, D),
            second(CG, D),
            whole(IB, D),
            whole(IB, 1),
            whole(IB // 2, D),
            whole(IB // 2, D),
            whole(IB, 1),
            whole(IB, 1),
            pl.BlockSpec((1, CG), lambda i: (0, i)),
        ],
        out_specs=[whole(D // 2, D), whole(D // 2, D), whole(8, 128)],
        out_shape=[
            jax.ShapeDtypeStruct((D // 2, D), BF),
            jax.ShapeDtypeStruct((D // 2, D), BF),
            jax.ShapeDtypeStruct((8, 128), F32),
        ],
        scratch_shapes=[
            pltpu.VMEM((16, 128), F32),
            pltpu.VMEM((IB, D), F32),
            pltpu.VMEM((D, D), F32),
        ],
        compiler_params=pltpu.CompilerParams(vmem_limit_bytes=32 << 20),
        cost_estimate=pl.CostEstimate(
            flops=2 * IB * D * 3 * QB + 2 * D * D * (QB + IB), bytes_accessed=9 << 20, transcendentals=IB * QB
        ),
        name="grads",
    )(core, order, parts, eqa, eqb, inva, invb, xqa, xqb, ei, invi, near, far, logc, ids, targets)


def body(xq_own, xi_own, weight, counts, positives):
    core, y, xh = lax.axis_index("c"), lax.axis_index("y"), lax.axis_index("xh")
    xl = lax.axis_index("xl")
    near = gather(xi_own, "z", 16).reshape(IB // 2, D)
    far = swap(near, "xl")
    two = jnp.concatenate([xq_own, swap(xq_own, "xh")])
    xqa = join(two, turn(two, 1), turn(two, 3), turn(two, 2), near)
    xqb = swap(xqa, "c")

    q = lax.iota(jnp.int32, 16)
    step = (q // 2) % 4
    from_y = (y + jnp.where(step == 1, 3, jnp.where(step == 2, 1, jnp.where(step == 3, 2, 0)))) % 4
    order = from_y * 4 + (xh ^ (q % 2)) * 2 + (core ^ (q // 8))
    picks = order[:, None, None] == q[None, :, None]
    targets = jnp.sum(jnp.where(picks, positives.reshape(1, 16, 128), 0), axis=1).reshape(1, QB)
    block = (y * 2 + xh) * 2 + core
    at = lax.iota(jnp.int32, IB)
    ids = ((at // 16) % 16 * 2 + (xl ^ (at // 256))) * 16 + at % 16
    logs = jnp.log(counts.astype(F32))
    logc = jnp.sum(jnp.where(ids[:, None] == at[None, :], logs[None, :], 0.0), axis=1, keepdims=True)
    ids = (block * IB + ids)[:, None]

    eqa, inva = tower(xqa, weight)
    eqb, invb = tower(xqb, weight)
    ei, invi, stat = score(order, eqa, eqb, weight, near, far, logc, ids, targets)
    parts = gather(stat, POOL, 16)
    send, keep, loss = grads(
        core.reshape(1), order, parts, eqa, eqb, inva, invb, xqa, xqb, ei, invi, near, far, logc, ids, targets
    )

    loss = (loss + swap(loss, "xl"))[0, 0] / ROWS
    s = (keep.astype(F32) + swap(send, "c").astype(F32)).astype(BF)
    s = jnp.sum(exchange(s.reshape(16, 24, D), YXX).astype(F32), axis=0).astype(BF)
    tail = jnp.zeros((7, 128), BF).at[0, :3].set(split3(loss))
    tail = jnp.broadcast_to(tail[None], (16, 7, 128))
    s = exchange(jnp.concatenate([s.reshape(16, 9, 128), tail], axis=1), "z")
    s = jnp.sum(s.astype(F32), axis=0)
    mean_loss = jnp.sum(s[9, :3])
    s = gather(s.astype(BF), "z", 16)[:, :9]
    s = gather(s.reshape(24, D), YXX, 16).reshape(D // 2, D)
    other = swap(s, "c")
    first, second = jnp.where(core == 0, s, other), jnp.where(core == 0, other, s)
    return mean_loss, jnp.concatenate([first, second]).astype(F32)


def solution(mesh):
    fine = Mesh(mesh.devices.reshape(4, 2, 2, 16, 2), ("y", "xh", "c", "z", "xl"))
    batch = ("z", "xl")
    return jax.shard_map(
        body,
        mesh=fine,
        in_specs=(P(batch + POOL, None), P(POOL + batch, None), P(), P(POOL), P(batch)),
        out_specs=(P(), P()),
        check_vma=False,
    )
```

```python
import functools

import jax
import jax.numpy as jnp
from jax import lax
from jax.experimental import pallas as pl
from jax.experimental.pallas import tpu as pltpu
from jax.sharding import Mesh, PartitionSpec as P

BF = jnp.bfloat16
F32 = jnp.float32
D = 768
YX = ("y", "xh")
YXX = ("y", "xh", "xl")
POOL = ("y", "xh", "c")
ROWS = 65536
QB = 2048
IB = 512
HALF = 1024
CH = 512
CG = 512
INV_NORM = 1.0 / ROWS**0.5
LOG2_NORM = -8.0
LOG2E = 1.4426950408889634


def swap(x, axis):
    return lax.ppermute(x, axis, [(0, 1), (1, 0)])


def turn(x, k):
    return lax.ppermute(x, "y", [(i, (i + k) % 4) for i in range(4)])


def exchange(x, axes):
    return lax.all_to_all(x, axes, 0, 0, tiled=True)


def gather(x, axes, n):
    return exchange(jnp.broadcast_to(x[None], (n,) + x.shape), axes)


def dot(a, b, dims):
    return lax.dot_general(a, b, (dims, ((), ())), preferred_element_type=F32)


def split3(x):
    hi = x.astype(BF)
    mid = (x - hi.astype(F32)).astype(BF)
    low = (x - hi.astype(F32) - mid.astype(F32)).astype(BF)
    return jnp.stack([hi, mid, low])


def unit_rows(x, weight):
    proj = dot(x, weight, ((1,), (0,)))
    inv = 1.0 / jnp.sqrt(jnp.sum(proj * proj, axis=1, keepdims=True) + 1e-06)
    return (proj * inv).astype(BF), inv


def score_tile(ei_ref, eq, logc_ref):
    return 100.0 * dot(ei_ref[...], eq, ((1,), (1,))) - logc_ref[...]


def whole(*s):
    return pl.BlockSpec(s, lambda i: (0,) * len(s))


def first(n, c):
    return pl.BlockSpec((n, c), lambda i: (jnp.minimum(i, HALF // n - 1), 0))


def second(n, c):
    return pl.BlockSpec((n, c), lambda i: (jnp.maximum(i - HALF // n, 0), 0))


def join_kernel(two_ref, a_ref, b_ref, c_ref, after_ref, out_ref):
    n = two_ref.shape[0]
    for k, ref in enumerate((two_ref, a_ref, b_ref, c_ref)):
        out_ref[k * n:(k + 1) * n, :] = ref[...]


def join(two, a, b, c, after):
    n = two.shape[0]
    return pl.pallas_call(
        join_kernel,
        in_specs=[pl.BlockSpec(memory_space=pltpu.VMEM)] * 4 + [pl.BlockSpec(memory_space=pl.ANY)],
        out_specs=pl.BlockSpec(memory_space=pltpu.VMEM),
        out_shape=jax.ShapeDtypeStruct((4 * n, D), BF),
        compiler_params=pltpu.CompilerParams(vmem_limit_bytes=8 << 20),
        cost_estimate=pl.CostEstimate(flops=0, bytes_accessed=16 * n * D, transcendentals=0),
        name="join",
    )(two, a, b, c, after)


def tower_kernel(x_ref, w_ref, e_ref, inv_ref):
    e_ref[...], inv_ref[...] = unit_rows(x_ref[...], w_ref[...])


def tower(x, weight):
    return pl.pallas_call(
        tower_kernel,
        grid=(HALF // CH,),
        in_specs=[pl.BlockSpec((CH, D), lambda i: (i, 0)), whole(D, D)],
        out_specs=[pl.BlockSpec((CH, D), lambda i: (i, 0)), pl.BlockSpec((CH, 1), lambda i: (i, 0))],
        out_shape=[pltpu.HBM((HALF, D), BF), pltpu.HBM((HALF, 1), F32)],
        compiler_params=pltpu.CompilerParams(vmem_limit_bytes=16 << 20),
        cost_estimate=pl.CostEstimate(flops=2 * HALF * D * D, bytes_accessed=4 * HALF * D, transcendentals=HALF),
        name="tower",
    )(x, weight)


def score_kernel(order_ref, eqa_ref, eqb_ref, w_ref, near_ref, far_ref, logc_ref, ids_ref, tgt_ref,
                 ei_ref, invi_ref, stat_ref):
    i = pl.program_id(0)

    @pl.when(i == 0)
    def _():
        for k, ref in enumerate((near_ref, far_ref)):
            part = slice(k * (IB // 2), (k + 1) * (IB // 2))
            ei_ref[part, :], invi_ref[part, :] = unit_rows(ref[...], w_ref[...])
        stat_ref[...] = jnp.zeros_like(stat_ref)

    def run(eq):
        scores = score_tile(ei_ref, eq, logc_ref)
        top = jnp.max(scores, axis=0, keepdims=True)
        lse = top + jnp.log(jnp.sum(jnp.exp(scores - top), axis=0, keepdims=True))
        pos = jnp.sum(jnp.where(ids_ref[...] == tgt_ref[...], scores, 0.0), axis=0, keepdims=True)
        for k in range(CH // 128):
            part = slice(k * 128, (k + 1) * 128)
            stat_ref[pl.ds(order_ref[i * (CH // 128) + k], 1), :] = lse[:, part]
            stat_ref[16:17, :] = stat_ref[16:17, :] + pos[:, part]

    @pl.when(i < HALF // CH)
    def _():
        run(eqa_ref[...])

    @pl.when(i >= HALF // CH)
    def _():
        run(eqb_ref[...])


def score(order, eqa, eqb, weight, near, far, logc, ids, targets):
    return pl.pallas_call(
        score_kernel,
        grid=(QB // CH,),
        in_specs=[
            pl.BlockSpec(memory_space=pltpu.SMEM),
            first(CH, D),
            second(CH, D),
            whole(D, D),
            whole(IB // 2, D),
            whole(IB // 2, D),
            whole(IB, 1),
            whole(IB, 1),
            pl.BlockSpec((1, CH), lambda i: (0, i)),
        ],
        out_specs=[whole(IB, D), whole(IB, 1), whole(24, 128)],
        out_shape=[
            jax.ShapeDtypeStruct((IB, D), BF),
            jax.ShapeDtypeStruct((IB, 1), F32),
            jax.ShapeDtypeStruct((24, 128), F32),
        ],
        compiler_params=pltpu.CompilerParams(vmem_limit_bytes=24 << 20),
        cost_estimate=pl.CostEstimate(
            flops=2 * IB * D * (D + QB), bytes_accessed=6 << 20, transcendentals=IB * QB
        ),
        name="score",
    )(order, eqa, eqb, weight, near, far, logc, ids, targets)


def grad_kernel(core_ref, order_ref, parts_ref, eqa_ref, eqb_ref, inva_ref, invb_ref, xqa_ref, xqb_ref,
                ei_ref, invi_ref, near_ref, far_ref, logc_ref, ids_ref, tgt_ref,
                send_ref, keep_ref, loss_ref, lse_ref, di_ref, acc_ref):
    i = pl.program_id(0)
    core = core_ref[0]

    @pl.when(i == 0)
    def _():
        vals = [parts_ref[d, :16, :] for d in range(16)]
        top = functools.reduce(jnp.maximum, vals)
        lse = top + jnp.log(sum(jnp.exp(v - top) for v in vals))
        lse_ref[...] = lse
        pos = sum(parts_ref[d, 16:17, :] for d in range(16))
        total = jnp.sum(jnp.sum(lse, axis=0, keepdims=True) - pos, axis=1, keepdims=True)
        loss_ref[...] = jnp.broadcast_to(total, (8, 128))
        di_ref[...] = jnp.zeros_like(di_ref)
        acc_ref[...] = jnp.zeros_like(acc_ref)

    def run(eq_ref, inv_ref, xq_ref):
        eq = eq_ref[...]
        rows = [order_ref[i * (CG // 128) + k] for k in range(CG // 128)]
        lse = jnp.concatenate([lse_ref[pl.ds(r, 1), :] for r in rows], axis=1)
        power = dot(ei_ref[...], eq, ((1,), (1,))) * (100.0 * LOG2E) - logc_ref[...] * LOG2E
        prob = jnp.exp2(power - (lse * LOG2E - LOG2_NORM))
        grad = jnp.where(ids_ref[...] == tgt_ref[...], prob - INV_NORM, prob).astype(BF)
        di_ref[...] += dot(grad, eq, ((1,), (0,)))
        dq = dot(grad, ei_ref[...], ((0,), (0,)))
        eq = eq.astype(F32)
        inner = jnp.sum(eq * dq, axis=1, keepdims=True)
        dz = ((dq - eq * inner) * (100.0 * inv_ref[...])).astype(BF)
        acc_ref[...] += dot(xq_ref[...], dz, ((0,), (0,)))

    @pl.when(i < HALF // CG)
    def _():
        run(eqa_ref, inva_ref, xqa_ref)

    @pl.when(i >= HALF // CG)
    def _():
        run(eqb_ref, invb_ref, xqb_ref)

    @pl.when(i == QB // CG - 1)
    def _():
        di = 100.0 * di_ref[...]
        ei = ei_ref[...].astype(F32)
        inner = jnp.sum(ei * di, axis=1, keepdims=True)
        dz = ((di - ei * inner) * invi_ref[...]).astype(BF)
        for k, ref in enumerate((near_ref, far_ref)):
            acc_ref[...] += dot(ref[...], dz[k * (IB // 2):(k + 1) * (IB // 2)], ((0,), (0,)))
        mine = pl.ds(pl.multiple_of(core * (D // 2), D // 2), D // 2)
        theirs = pl.ds(pl.multiple_of((1 - core) * (D // 2), D // 2), D // 2)
        keep_ref[...] = acc_ref[mine, :].astype(BF)
        send_ref[...] = acc_ref[theirs, :].astype(BF)


def grads(core, order, parts, eqa, eqb, inva, invb, xqa, xqb, ei, invi, near, far, logc, ids, targets):
    return pl.pallas_call(
        grad_kernel,
        grid=(QB // CG,),
        in_specs=[
            pl.BlockSpec(memory_space=pltpu.SMEM),
            pl.BlockSpec(memory_space=pltpu.SMEM),
            whole(16, 24, 128),
            first(CG, D),
            second(CG, D),
            first(CG, 1),
            second(CG, 1),
            first(CG, D),
            second(CG, D),
            whole(IB, D),
            whole(IB, 1),
            whole(IB // 2, D),
            whole(IB // 2, D),
            whole(IB, 1),
            whole(IB, 1),
            pl.BlockSpec((1, CG), lambda i: (0, i)),
        ],
        out_specs=[whole(D // 2, D), whole(D // 2, D), whole(8, 128)],
        out_shape=[
            jax.ShapeDtypeStruct((D // 2, D), BF),
            jax.ShapeDtypeStruct((D // 2, D), BF),
            jax.ShapeDtypeStruct((8, 128), F32),
        ],
        scratch_shapes=[
            pltpu.VMEM((16, 128), F32),
            pltpu.VMEM((IB, D), F32),
            pltpu.VMEM((D, D), F32),
        ],
        compiler_params=pltpu.CompilerParams(vmem_limit_bytes=32 << 20),
        cost_estimate=pl.CostEstimate(
            flops=2 * IB * D * 3 * QB + 2 * D * D * (QB + IB), bytes_accessed=9 << 20, transcendentals=IB * QB
        ),
        name="grads",
    )(core, order, parts, eqa, eqb, inva, invb, xqa, xqb, ei, invi, near, far, logc, ids, targets)


def body(xq_own, xi_own, weight, counts, positives):
    core, y, xh = lax.axis_index("c"), lax.axis_index("y"), lax.axis_index("xh")
    xl = lax.axis_index("xl")
    near = gather(xi_own, "z", 16).reshape(IB // 2, D)
    far = swap(near, "xl")
    two = jnp.concatenate([xq_own, swap(xq_own, "xh")])
    xqa = join(two, turn(two, 1), turn(two, 3), turn(two, 2), far)
    xqb = swap(xqa, "c")

    q = lax.iota(jnp.int32, 16)
    step = (q // 2) % 4
    from_y = (y + jnp.where(step == 1, 3, jnp.where(step == 2, 1, jnp.where(step == 3, 2, 0)))) % 4
    order = from_y * 4 + (xh ^ (q % 2)) * 2 + (core ^ (q // 8))
    picks = order[:, None, None] == q[None, :, None]
    targets = jnp.sum(jnp.where(picks, positives.reshape(1, 16, 128), 0), axis=1).reshape(1, QB)
    block = (y * 2 + xh) * 2 + core
    at = lax.iota(jnp.int32, IB)
    ids = ((at // 16) % 16 * 2 + (xl ^ (at // 256))) * 16 + at % 16
    logs = jnp.log(counts.astype(F32))
    logc = jnp.sum(jnp.where(ids[:, None] == at[None, :], logs[None, :], 0.0), axis=1, keepdims=True)
    ids = (block * IB + ids)[:, None]

    eqa, inva = tower(xqa, weight)
    eqb, invb = tower(xqb, weight)
    ei, invi, stat = score(order, eqa, eqb, weight, near, far, logc, ids, targets)
    parts = gather(stat, POOL, 16)
    send, keep, loss = grads(
        core.reshape(1), order, parts, eqa, eqb, inva, invb, xqa, xqb, ei, invi, near, far, logc, ids, targets
    )

    loss = (loss + swap(loss, "xl"))[0, 0] / ROWS
    s = (keep.astype(F32) + swap(send, "c").astype(F32)).astype(BF)
    s = jnp.sum(exchange(s.reshape(16, 24, D), YXX).astype(F32), axis=0).astype(BF)
    tail = jnp.zeros((7, 128), BF).at[0, :3].set(split3(loss))
    tail = jnp.broadcast_to(tail[None], (16, 7, 128))
    s = exchange(jnp.concatenate([s.reshape(16, 9, 128), tail], axis=1), "z")
    s = jnp.sum(s.astype(F32), axis=0)
    mean_loss = jnp.sum(s[9, :3])
    s = gather(s.astype(BF), "z", 16)[:, :9]
    s = gather(s.reshape(24, D), YXX, 16).reshape(D // 2, D)
    other = swap(s, "c")
    first, second = jnp.where(core == 0, s, other), jnp.where(core == 0, other, s)
    return mean_loss, jnp.concatenate([first, second]).astype(F32)


def solution(mesh):
    fine = Mesh(mesh.devices.reshape(4, 2, 2, 16, 2), ("y", "xh", "c", "z", "xl"))
    batch = ("z", "xl")
    return jax.shard_map(
        body,
        mesh=fine,
        in_specs=(P(batch + POOL, None), P(POOL + batch, None), P(), P(POOL), P(batch)),
        out_specs=(P(), P()),
        check_vma=False,
    )
```

```python
import functools

import jax
import jax.numpy as jnp
from jax import lax
from jax.experimental import pallas as pl
from jax.experimental.pallas import tpu as pltpu
from jax.sharding import Mesh, PartitionSpec as P

BF = jnp.bfloat16
F32 = jnp.float32
D = 768
YX = ("y", "xh")
YXX = ("y", "xh", "xl")
POOL = ("y", "xh", "c")
ROWS = 65536
QB = 2048
IB = 512
HALF = 1024
CH = 512
CG = 512
INV_NORM = 1.0 / ROWS**0.5
LOG2_NORM = -8.0
LOG2E = 1.4426950408889634


def swap(x, axis):
    return lax.ppermute(x, axis, [(0, 1), (1, 0)])


def turn(x, k):
    return lax.ppermute(x, "y", [(i, (i + k) % 4) for i in range(4)])


def exchange(x, axes):
    return lax.all_to_all(x, axes, 0, 0, tiled=True)


def gather(x, axes, n):
    return exchange(jnp.broadcast_to(x[None], (n,) + x.shape), axes)


def dot(a, b, dims):
    return lax.dot_general(a, b, (dims, ((), ())), preferred_element_type=F32)


def split3(x):
    hi = x.astype(BF)
    mid = (x - hi.astype(F32)).astype(BF)
    low = (x - hi.astype(F32) - mid.astype(F32)).astype(BF)
    return jnp.stack([hi, mid, low])


def unit_rows(x, weight):
    proj = dot(x, weight, ((1,), (0,)))
    inv = 1.0 / jnp.sqrt(jnp.sum(proj * proj, axis=1, keepdims=True) + 1e-06)
    return (proj * inv).astype(BF), inv


def score_tile(ei_ref, eq, logc_ref):
    return 100.0 * dot(ei_ref[...], eq, ((1,), (1,))) - logc_ref[...]


def whole(*s):
    return pl.BlockSpec(s, lambda i: (0,) * len(s))


def first(n, c):
    return pl.BlockSpec((n, c), lambda i: (jnp.minimum(i, HALF // n - 1), 0))


def second(n, c):
    return pl.BlockSpec((n, c), lambda i: (jnp.maximum(i - HALF // n, 0), 0))


def join_kernel(two_ref, a_ref, b_ref, c_ref, after_ref, out_ref):
    n = two_ref.shape[0]
    for k, ref in enumerate((two_ref, a_ref, b_ref, c_ref)):
        out_ref[k * n:(k + 1) * n, :] = ref[...]


def join(two, a, b, c, after):
    n = two.shape[0]
    return pl.pallas_call(
        join_kernel,
        in_specs=[pl.BlockSpec(memory_space=pltpu.VMEM)] * 4 + [pl.BlockSpec(memory_space=pl.ANY)],
        out_specs=pl.BlockSpec(memory_space=pltpu.VMEM),
        out_shape=jax.ShapeDtypeStruct((4 * n, D), BF),
        compiler_params=pltpu.CompilerParams(vmem_limit_bytes=8 << 20),
        cost_estimate=pl.CostEstimate(flops=0, bytes_accessed=16 * n * D, transcendentals=0),
        name="join",
    )(two, a, b, c, after)


def score_step(base, order_ref, x_ref, w_ref, ei_ref, logc_ref, ids_ref, tgt_ref, eq_ref, inv_ref, stat_ref):
    eq, inv_ref[...] = unit_rows(x_ref[...], w_ref[...])
    eq_ref[...] = eq
    scores = score_tile(ei_ref, eq, logc_ref)
    top = jnp.max(scores, axis=0, keepdims=True)
    lse = top + jnp.log(jnp.sum(jnp.exp(scores - top), axis=0, keepdims=True))
    pos = jnp.sum(jnp.where(ids_ref[...] == tgt_ref[...], scores, 0.0), axis=0, keepdims=True)
    for k in range(CH // 128):
        row = order_ref[base + pl.program_id(0) * (CH // 128) + k]
        part = slice(k * 128, (k + 1) * 128)
        stat_ref[pl.ds(row, 1), :] = lse[:, part]
        stat_ref[16:17, :] = stat_ref[16:17, :] + pos[:, part]


def first_kernel(order_ref, x_ref, w_ref, near_ref, far_ref, logc_ref, ids_ref, tgt_ref,
                 eq_ref, inv_ref, ei_ref, invi_ref, stat_ref):
    @pl.when(pl.program_id(0) == 0)
    def _():
        for k, ref in enumerate((near_ref, far_ref)):
            part = slice(k * (IB // 2), (k + 1) * (IB // 2))
            ei_ref[part, :], invi_ref[part, :] = unit_rows(ref[...], w_ref[...])
        stat_ref[...] = jnp.zeros_like(stat_ref)

    score_step(0, order_ref, x_ref, w_ref, ei_ref, logc_ref, ids_ref, tgt_ref, eq_ref, inv_ref, stat_ref)


def second_kernel(order_ref, x_ref, w_ref, ei_ref, logc_ref, ids_ref, tgt_ref, before_ref,
                  eq_ref, inv_ref, stat_ref):
    @pl.when(pl.program_id(0) == 0)
    def _():
        stat_ref[...] = before_ref[...]

    score_step(8, order_ref, x_ref, w_ref, ei_ref, logc_ref, ids_ref, tgt_ref, eq_ref, inv_ref, stat_ref)


def score_call(kernel, base, items, item_specs, item_shapes, order, x, weight, side, targets, tail, name):
    steps = HALF // CH
    return pl.pallas_call(
        kernel,
        grid=(steps,),
        in_specs=[
            pl.BlockSpec(memory_space=pltpu.SMEM),
            pl.BlockSpec((CH, D), lambda i: (i, 0)),
            whole(D, D),
            *[whole(*x.shape) for x in items],
            whole(IB, 1),
            whole(IB, 1),
            pl.BlockSpec((1, CH), lambda i: (0, i + base * steps)),
        ]
        + [whole(24, 128)] * len(tail),
        out_specs=[
            pl.BlockSpec((CH, D), lambda i: (i, 0)),
            pl.BlockSpec((CH, 1), lambda i: (i, 0)),
            *item_specs,
            whole(24, 128),
        ],
        out_shape=[
            jax.ShapeDtypeStruct((HALF, D), BF),
            jax.ShapeDtypeStruct((HALF, 1), F32),
            *item_shapes,
            jax.ShapeDtypeStruct((24, 128), F32),
        ],
        compiler_params=pltpu.CompilerParams(vmem_limit_bytes=24 << 20),
        cost_estimate=pl.CostEstimate(
            flops=2 * HALF * D * (D + IB), bytes_accessed=6 << 20, transcendentals=IB * HALF
        ),
        name=name,
    )(order, x, weight, *items, *side, targets, *tail)


def grad_kernel(core_ref, order_ref, parts_ref, eqa_ref, eqb_ref, inva_ref, invb_ref, xqa_ref, xqb_ref,
                ei_ref, invi_ref, near_ref, far_ref, logc_ref, ids_ref, tgt_ref,
                send_ref, keep_ref, loss_ref, lse_ref, di_ref, acc_ref):
    i = pl.program_id(0)
    core = core_ref[0]

    @pl.when(i == 0)
    def _():
        vals = [parts_ref[d, :16, :] for d in range(16)]
        top = functools.reduce(jnp.maximum, vals)
        lse = top + jnp.log(sum(jnp.exp(v - top) for v in vals))
        lse_ref[...] = lse
        pos = sum(parts_ref[d, 16:17, :] for d in range(16))
        total = jnp.sum(jnp.sum(lse, axis=0, keepdims=True) - pos, axis=1, keepdims=True)
        loss_ref[...] = jnp.broadcast_to(total, (8, 128))
        di_ref[...] = jnp.zeros_like(di_ref)
        acc_ref[...] = jnp.zeros_like(acc_ref)

    def run(eq_ref, inv_ref, xq_ref):
        eq = eq_ref[...]
        rows = [order_ref[i * (CG // 128) + k] for k in range(CG // 128)]
        lse = jnp.concatenate([lse_ref[pl.ds(r, 1), :] for r in rows], axis=1)
        power = dot(ei_ref[...], eq, ((1,), (1,))) * (100.0 * LOG2E) - logc_ref[...] * LOG2E
        prob = jnp.exp2(power - (lse * LOG2E - LOG2_NORM))
        grad = jnp.where(ids_ref[...] == tgt_ref[...], prob - INV_NORM, prob).astype(BF)
        di_ref[...] += dot(grad, eq, ((1,), (0,)))
        dq = dot(grad, ei_ref[...], ((0,), (0,)))
        eq = eq.astype(F32)
        inner = jnp.sum(eq * dq, axis=1, keepdims=True)
        dz = ((dq - eq * inner) * (100.0 * inv_ref[...])).astype(BF)
        acc_ref[...] += dot(xq_ref[...], dz, ((0,), (0,)))

    @pl.when(i < HALF // CG)
    def _():
        run(eqa_ref, inva_ref, xqa_ref)

    @pl.when(i >= HALF // CG)
    def _():
        run(eqb_ref, invb_ref, xqb_ref)

    @pl.when(i == QB // CG - 1)
    def _():
        di = 100.0 * di_ref[...]
        ei = ei_ref[...].astype(F32)
        inner = jnp.sum(ei * di, axis=1, keepdims=True)
        dz = ((di - ei * inner) * invi_ref[...]).astype(BF)
        for k, ref in enumerate((near_ref, far_ref)):
            acc_ref[...] += dot(ref[...], dz[k * (IB // 2):(k + 1) * (IB // 2)], ((0,), (0,)))
        mine = pl.ds(pl.multiple_of(core * (D // 2), D // 2), D // 2)
        theirs = pl.ds(pl.multiple_of((1 - core) * (D // 2), D // 2), D // 2)
        keep_ref[...] = acc_ref[mine, :].astype(BF)
        send_ref[...] = acc_ref[theirs, :].astype(BF)


def grads(core, order, parts, eqa, eqb, inva, invb, xqa, xqb, ei, invi, near, far, logc, ids, targets):
    return pl.pallas_call(
        grad_kernel,
        grid=(QB // CG,),
        in_specs=[
            pl.BlockSpec(memory_space=pltpu.SMEM),
            pl.BlockSpec(memory_space=pltpu.SMEM),
            whole(16, 24, 128),
            first(CG, D),
            second(CG, D),
            first(CG, 1),
            second(CG, 1),
            first(CG, D),
            second(CG, D),
            whole(IB, D),
            whole(IB, 1),
            whole(IB // 2, D),
            whole(IB // 2, D),
            whole(IB, 1),
            whole(IB, 1),
            pl.BlockSpec((1, CG), lambda i: (0, i)),
        ],
        out_specs=[whole(D // 2, D), whole(D // 2, D), whole(8, 128)],
        out_shape=[
            jax.ShapeDtypeStruct((D // 2, D), BF),
            jax.ShapeDtypeStruct((D // 2, D), BF),
            jax.ShapeDtypeStruct((8, 128), F32),
        ],
        scratch_shapes=[
            pltpu.VMEM((16, 128), F32),
            pltpu.VMEM((IB, D), F32),
            pltpu.VMEM((D, D), F32),
        ],
        compiler_params=pltpu.CompilerParams(vmem_limit_bytes=32 << 20),
        cost_estimate=pl.CostEstimate(
            flops=2 * IB * D * 3 * QB + 2 * D * D * (QB + IB), bytes_accessed=9 << 20, transcendentals=IB * QB
        ),
        name="grads",
    )(core, order, parts, eqa, eqb, inva, invb, xqa, xqb, ei, invi, near, far, logc, ids, targets)


def body(xq_own, xi_own, weight, counts, positives):
    core, y, xh = lax.axis_index("c"), lax.axis_index("y"), lax.axis_index("xh")
    xl = lax.axis_index("xl")
    near = gather(xi_own, "z", 16).reshape(IB // 2, D)
    far = swap(near, "xl")
    two = jnp.concatenate([xq_own, swap(xq_own, "xh")])
    xqa = join(two, turn(two, 1), turn(two, 3), turn(two, 2), far)
    xqb = swap(xqa, "c")

    q = lax.iota(jnp.int32, 16)
    step = (q // 2) % 4
    from_y = (y + jnp.where(step == 1, 3, jnp.where(step == 2, 1, jnp.where(step == 3, 2, 0)))) % 4
    order = from_y * 4 + (xh ^ (q % 2)) * 2 + (core ^ (q // 8))
    picks = order[:, None, None] == q[None, :, None]
    targets = jnp.sum(jnp.where(picks, positives.reshape(1, 16, 128), 0), axis=1).reshape(1, QB)
    block = (y * 2 + xh) * 2 + core
    at = lax.iota(jnp.int32, IB)
    ids = ((at // 16) % 16 * 2 + (xl ^ (at // 256))) * 16 + at % 16
    logs = jnp.log(counts.astype(F32))
    logc = jnp.sum(jnp.where(ids[:, None] == at[None, :], logs[None, :], 0.0), axis=1, keepdims=True)
    ids = (block * IB + ids)[:, None]

    eqa, inva, ei, invi, stat = score_call(
        first_kernel,
        0,
        (near, far),
        [whole(IB, D), whole(IB, 1)],
        [jax.ShapeDtypeStruct((IB, D), BF), jax.ShapeDtypeStruct((IB, 1), F32)],
        order, xqa, weight, (logc, ids), targets, (), "score_first",
    )
    eqb, invb, stat = score_call(
        second_kernel, 1, (ei,), [], [], order, xqb, weight, (logc, ids), targets, (stat,), "score_second"
    )
    parts = gather(stat, POOL, 16)
    send, keep, loss = grads(
        core.reshape(1), order, parts, eqa, eqb, inva, invb, xqa, xqb, ei, invi, near, far, logc, ids, targets
    )

    loss = (loss + swap(loss, "xl"))[0, 0] / ROWS
    s = (keep.astype(F32) + swap(send, "c").astype(F32)).astype(BF)
    s = jnp.sum(exchange(s.reshape(16, 24, D), YXX).astype(F32), axis=0).astype(BF)
    tail = jnp.zeros((7, 128), BF).at[0, :3].set(split3(loss))
    tail = jnp.broadcast_to(tail[None], (16, 7, 128))
    s = exchange(jnp.concatenate([s.reshape(16, 9, 128), tail], axis=1), "z")
    s = jnp.sum(s.astype(F32), axis=0)
    mean_loss = jnp.sum(s[9, :3])
    s = gather(s.astype(BF), "z", 16)[:, :9]
    s = gather(s.reshape(24, D), YXX, 16).reshape(D // 2, D)
    other = swap(s, "c")
    first, second = jnp.where(core == 0, s, other), jnp.where(core == 0, other, s)
    return mean_loss, jnp.concatenate([first, second]).astype(F32)


def solution(mesh):
    fine = Mesh(mesh.devices.reshape(4, 2, 2, 16, 2), ("y", "xh", "c", "z", "xl"))
    batch = ("z", "xl")
    return jax.shard_map(
        body,
        mesh=fine,
        in_specs=(P(batch + POOL, None), P(POOL + batch, None), P(), P(POOL), P(batch)),
        out_specs=(P(), P()),
        check_vma=False,
    )
```

```python
import functools

import jax
import jax.numpy as jnp
from jax import lax
from jax.experimental import pallas as pl
from jax.experimental.pallas import tpu as pltpu
from jax.sharding import Mesh, PartitionSpec as P

BF = jnp.bfloat16
F32 = jnp.float32
D = 768
YX = ("y", "xh")
YXX = ("y", "xh", "xl")
POOL = ("y", "xh", "c")
ROWS = 65536
QB = 2048
IB = 512
HALF = 1024
CH = 512
CG = 512
INV_NORM = 1.0 / ROWS**0.5
LOG2_NORM = -8.0
LOG2E = 1.4426950408889634


def swap(x, axis):
    return lax.ppermute(x, axis, [(0, 1), (1, 0)])


def turn(x, k):
    return lax.ppermute(x, "y", [(i, (i + k) % 4) for i in range(4)])


def exchange(x, axes):
    return lax.all_to_all(x, axes, 0, 0, tiled=True)


def gather(x, axes, n):
    return exchange(jnp.broadcast_to(x[None], (n,) + x.shape), axes)


def dot(a, b, dims):
    return lax.dot_general(a, b, (dims, ((), ())), preferred_element_type=F32)


def split3(x):
    hi = x.astype(BF)
    mid = (x - hi.astype(F32)).astype(BF)
    low = (x - hi.astype(F32) - mid.astype(F32)).astype(BF)
    return jnp.stack([hi, mid, low])


def unit_rows(x, weight):
    proj = dot(x, weight, ((1,), (0,)))
    inv = 1.0 / jnp.sqrt(jnp.sum(proj * proj, axis=1, keepdims=True) + 1e-06)
    return (proj * inv).astype(BF), inv


def score_tile(ei_ref, eq, logc_ref):
    return 100.0 * dot(ei_ref[...], eq, ((1,), (1,))) - logc_ref[...]


def whole(*s):
    return pl.BlockSpec(s, lambda i: (0,) * len(s))


def first(n, c):
    return pl.BlockSpec((n, c), lambda i: (jnp.minimum(i, HALF // n - 1), 0))


def second(n, c):
    return pl.BlockSpec((n, c), lambda i: (jnp.maximum(i - HALF // n, 0), 0))


def join_kernel(two_ref, a_ref, b_ref, c_ref, after_ref, out_ref):
    n = two_ref.shape[0]
    for k, ref in enumerate((two_ref, a_ref, b_ref, c_ref)):
        out_ref[k * n:(k + 1) * n, :] = ref[...]


def join(two, a, b, c, after):
    n = two.shape[0]
    return pl.pallas_call(
        join_kernel,
        in_specs=[pl.BlockSpec(memory_space=pltpu.VMEM)] * 4 + [pl.BlockSpec(memory_space=pl.ANY)],
        out_specs=pl.BlockSpec(memory_space=pltpu.VMEM),
        out_shape=jax.ShapeDtypeStruct((4 * n, D), BF),
        compiler_params=pltpu.CompilerParams(vmem_limit_bytes=8 << 20),
        cost_estimate=pl.CostEstimate(flops=0, bytes_accessed=16 * n * D, transcendentals=0),
        name="join",
    )(two, a, b, c, after)


def score_step(base, order_ref, x_ref, w_ref, ei_ref, logc_ref, ids_ref, tgt_ref, eq_ref, inv_ref, stat_ref):
    eq, inv_ref[...] = unit_rows(x_ref[...], w_ref[...])
    eq_ref[...] = eq
    scores = score_tile(ei_ref, eq, logc_ref)
    top = jnp.max(scores, axis=0, keepdims=True)
    lse = top + jnp.log(jnp.sum(jnp.exp(scores - top), axis=0, keepdims=True))
    pos = jnp.sum(jnp.where(ids_ref[...] == tgt_ref[...], scores, 0.0), axis=0, keepdims=True)
    for k in range(CH // 128):
        row = order_ref[base + pl.program_id(0) * (CH // 128) + k]
        part = slice(k * 128, (k + 1) * 128)
        stat_ref[pl.ds(row, 1), :] = lse[:, part]
        stat_ref[16:17, :] = stat_ref[16:17, :] + pos[:, part]


def first_kernel(order_ref, x_ref, w_ref, near_ref, far_ref, logc_ref, ids_ref, tgt_ref,
                 eq_ref, inv_ref, ei_ref, invi_ref, stat_ref):
    @pl.when(pl.program_id(0) == 0)
    def _():
        for k, ref in enumerate((near_ref, far_ref)):
            part = slice(k * (IB // 2), (k + 1) * (IB // 2))
            ei_ref[part, :], invi_ref[part, :] = unit_rows(ref[...], w_ref[...])
        stat_ref[...] = jnp.zeros_like(stat_ref)

    score_step(0, order_ref, x_ref, w_ref, ei_ref, logc_ref, ids_ref, tgt_ref, eq_ref, inv_ref, stat_ref)


def second_kernel(order_ref, x_ref, w_ref, ei_ref, logc_ref, ids_ref, tgt_ref, before_ref,
                  eq_ref, inv_ref, stat_ref):
    @pl.when(pl.program_id(0) == 0)
    def _():
        stat_ref[...] = before_ref[...]

    score_step(8, order_ref, x_ref, w_ref, ei_ref, logc_ref, ids_ref, tgt_ref, eq_ref, inv_ref, stat_ref)


def score_call(kernel, base, items, item_specs, item_shapes, order, x, weight, side, targets, tail, name):
    steps = HALF // CH
    return pl.pallas_call(
        kernel,
        grid=(steps,),
        in_specs=[
            pl.BlockSpec(memory_space=pltpu.SMEM),
            pl.BlockSpec((CH, D), lambda i: (i, 0)),
            whole(D, D),
            *[whole(*x.shape) for x in items],
            whole(IB, 1),
            whole(IB, 1),
            pl.BlockSpec((1, CH), lambda i: (0, i + base * steps)),
        ]
        + [whole(24, 128)] * len(tail),
        out_specs=[
            pl.BlockSpec((CH, D), lambda i: (i, 0)),
            pl.BlockSpec((CH, 1), lambda i: (i, 0)),
            *item_specs,
            whole(24, 128),
        ],
        out_shape=[
            jax.ShapeDtypeStruct((HALF, D), BF),
            jax.ShapeDtypeStruct((HALF, 1), F32),
            *item_shapes,
            jax.ShapeDtypeStruct((24, 128), F32),
        ],
        compiler_params=pltpu.CompilerParams(vmem_limit_bytes=24 << 20),
        cost_estimate=pl.CostEstimate(
            flops=2 * HALF * D * (D + IB), bytes_accessed=6 << 20, transcendentals=IB * HALF
        ),
        name=name,
    )(order, x, weight, *items, *side, targets, *tail)


def grad_kernel(core_ref, order_ref, parts_ref, eqa_ref, eqb_ref, inva_ref, invb_ref, xqa_ref, xqb_ref,
                ei_ref, invi_ref, near_ref, far_ref, logc_ref, ids_ref, tgt_ref,
                send_ref, keep_ref, loss_ref, lse_ref, di_ref, acc_ref):
    i = pl.program_id(0)
    core = core_ref[0]

    @pl.when(i == 0)
    def _():
        vals = [parts_ref[d, :16, :] for d in range(16)]
        top = functools.reduce(jnp.maximum, vals)
        lse = top + jnp.log(sum(jnp.exp(v - top) for v in vals))
        lse_ref[...] = lse
        pos = sum(parts_ref[d, 16:17, :] for d in range(16))
        total = jnp.sum(jnp.sum(lse, axis=0, keepdims=True) - pos, axis=1, keepdims=True)
        loss_ref[...] = jnp.broadcast_to(total, (8, 128))
        di_ref[...] = jnp.zeros_like(di_ref)
        acc_ref[...] = jnp.zeros_like(acc_ref)

    def run(eq_ref, inv_ref, xq_ref):
        eq = eq_ref[...]
        rows = [order_ref[i * (CG // 128) + k] for k in range(CG // 128)]
        lse = jnp.concatenate([lse_ref[pl.ds(r, 1), :] for r in rows], axis=1)
        power = dot(ei_ref[...], eq, ((1,), (1,))) * (100.0 * LOG2E) - logc_ref[...] * LOG2E
        prob = jnp.exp2(power - (lse * LOG2E - LOG2_NORM))
        grad = jnp.where(ids_ref[...] == tgt_ref[...], prob - INV_NORM, prob).astype(BF)
        di_ref[...] += dot(grad, eq, ((1,), (0,)))
        dq = dot(grad, ei_ref[...], ((0,), (0,)))
        eq = eq.astype(F32)
        inner = jnp.sum(eq * dq, axis=1, keepdims=True)
        dz = ((dq - eq * inner) * (100.0 * inv_ref[...])).astype(BF)
        acc_ref[...] += dot(xq_ref[...], dz, ((0,), (0,)))

    @pl.when(i < HALF // CG)
    def _():
        run(eqa_ref, inva_ref, xqa_ref)

    @pl.when(i >= HALF // CG)
    def _():
        run(eqb_ref, invb_ref, xqb_ref)

    @pl.when(i == QB // CG - 1)
    def _():
        di = 100.0 * di_ref[...]
        ei = ei_ref[...].astype(F32)
        inner = jnp.sum(ei * di, axis=1, keepdims=True)
        dz = ((di - ei * inner) * invi_ref[...]).astype(BF)
        for k, ref in enumerate((near_ref, far_ref)):
            acc_ref[...] += dot(ref[...], dz[k * (IB // 2):(k + 1) * (IB // 2)], ((0,), (0,)))
        mine = pl.ds(pl.multiple_of(core * (D // 2), D // 2), D // 2)
        theirs = pl.ds(pl.multiple_of((1 - core) * (D // 2), D // 2), D // 2)
        keep_ref[...] = acc_ref[mine, :].astype(BF)
        send_ref[...] = acc_ref[theirs, :].astype(BF)


def grads(core, order, parts, eqa, eqb, inva, invb, xqa, xqb, ei, invi, near, far, logc, ids, targets):
    return pl.pallas_call(
        grad_kernel,
        grid=(QB // CG,),
        in_specs=[
            pl.BlockSpec(memory_space=pltpu.SMEM),
            pl.BlockSpec(memory_space=pltpu.SMEM),
            whole(16, 24, 128),
            first(CG, D),
            second(CG, D),
            first(CG, 1),
            second(CG, 1),
            first(CG, D),
            second(CG, D),
            whole(IB, D),
            whole(IB, 1),
            whole(IB // 2, D),
            whole(IB // 2, D),
            whole(IB, 1),
            whole(IB, 1),
            pl.BlockSpec((1, CG), lambda i: (0, i)),
        ],
        out_specs=[whole(D // 2, D), whole(D // 2, D), whole(8, 128)],
        out_shape=[
            jax.ShapeDtypeStruct((D // 2, D), BF),
            jax.ShapeDtypeStruct((D // 2, D), BF),
            jax.ShapeDtypeStruct((8, 128), F32),
        ],
        scratch_shapes=[
            pltpu.VMEM((16, 128), F32),
            pltpu.VMEM((IB, D), F32),
            pltpu.VMEM((D, D), F32),
        ],
        compiler_params=pltpu.CompilerParams(vmem_limit_bytes=32 << 20),
        cost_estimate=pl.CostEstimate(
            flops=2 * IB * D * 3 * QB + 2 * D * D * (QB + IB), bytes_accessed=9 << 20, transcendentals=IB * QB
        ),
        name="grads",
    )(core, order, parts, eqa, eqb, inva, invb, xqa, xqb, ei, invi, near, far, logc, ids, targets)


def body(xq_own, xi_own, weight, counts, positives):
    core, y, xh = lax.axis_index("c"), lax.axis_index("y"), lax.axis_index("xh")
    xl = lax.axis_index("xl")
    near = gather(xi_own, "z", 16).reshape(IB // 2, D)
    far = swap(near, "xl")
    two = jnp.concatenate([xq_own, swap(xq_own, "xh")])
    xqa = join(two, turn(two, 1), turn(two, 3), turn(two, 2), far)
    xqb = swap(xqa, "c")

    q = lax.iota(jnp.int32, 16)
    step = (q // 2) % 4
    from_y = (y + jnp.where(step == 1, 3, jnp.where(step == 2, 1, jnp.where(step == 3, 2, 0)))) % 4
    order = from_y * 4 + (xh ^ (q % 2)) * 2 + (core ^ (q // 8))
    picks = order[:, None, None] == q[None, :, None]
    targets = jnp.sum(jnp.where(picks, positives.reshape(1, 16, 128), 0), axis=1).reshape(1, QB)
    block = (y * 2 + xh) * 2 + core
    weight, near = pltpu.with_memory_space_constraint(weight, pltpu.HBM), pltpu.with_memory_space_constraint(near, pltpu.HBM)
    at = lax.iota(jnp.int32, IB)
    ids = ((at // 16) % 16 * 2 + (xl ^ (at // 256))) * 16 + at % 16
    logs = jnp.log(counts.astype(F32))
    logc = jnp.sum(jnp.where(ids[:, None] == at[None, :], logs[None, :], 0.0), axis=1, keepdims=True)
    ids = (block * IB + ids)[:, None]

    eqa, inva, ei, invi, stat = score_call(
        first_kernel,
        0,
        (near, far),
        [whole(IB, D), whole(IB, 1)],
        [jax.ShapeDtypeStruct((IB, D), BF), jax.ShapeDtypeStruct((IB, 1), F32)],
        order, xqa, weight, (logc, ids), targets, (), "score_first",
    )
    eqb, invb, stat = score_call(
        second_kernel, 1, (ei,), [], [], order, xqb, weight, (logc, ids), targets, (stat,), "score_second"
    )
    parts = gather(stat, POOL, 16)
    send, keep, loss = grads(
        core.reshape(1), order, parts, eqa, eqb, inva, invb, xqa, xqb, ei, invi, near, far, logc, ids, targets
    )

    loss = (loss + swap(loss, "xl"))[0, 0] / ROWS
    s = (keep.astype(F32) + swap(send, "c").astype(F32)).astype(BF)
    s = jnp.sum(exchange(s.reshape(16, 24, D), YXX).astype(F32), axis=0).astype(BF)
    tail = jnp.zeros((7, 128), BF).at[0, :3].set(split3(loss))
    tail = jnp.broadcast_to(tail[None], (16, 7, 128))
    s = exchange(jnp.concatenate([s.reshape(16, 9, 128), tail], axis=1), "z")
    s = jnp.sum(s.astype(F32), axis=0)
    mean_loss = jnp.sum(s[9, :3])
    s = gather(s.astype(BF), "z", 16)[:, :9]
    s = gather(s.reshape(24, D), YXX, 16).reshape(D // 2, D)
    other = swap(s, "c")
    first, second = jnp.where(core == 0, s, other), jnp.where(core == 0, other, s)
    return mean_loss, jnp.concatenate([first, second]).astype(F32)


def solution(mesh):
    fine = Mesh(mesh.devices.reshape(4, 2, 2, 16, 2), ("y", "xh", "c", "z", "xl"))
    batch = ("z", "xl")
    return jax.shard_map(
        body,
        mesh=fine,
        in_specs=(P(batch + POOL, None), P(POOL + batch, None), P(), P(POOL), P(batch)),
        out_specs=(P(), P()),
        check_vma=False,
    )
```

```python
import functools

import jax
import jax.numpy as jnp
from jax import lax
from jax.experimental import pallas as pl
from jax.experimental.pallas import tpu as pltpu
from jax.sharding import Mesh, PartitionSpec as P

BF = jnp.bfloat16
F32 = jnp.float32
D = 768
YX = ("y", "xh")
YXX = ("y", "xh", "xl")
POOL = ("y", "xh", "c")
ROWS = 65536
QB = 2048
IB = 512
HALF = 1024
CH = 512
CG = 512
INV_NORM = 1.0 / ROWS**0.5
LOG2_NORM = -8.0
LOG2E = 1.4426950408889634


def swap(x, axis):
    return lax.ppermute(x, axis, [(0, 1), (1, 0)])


def turn(x, k):
    return lax.ppermute(x, "y", [(i, (i + k) % 4) for i in range(4)])


def exchange(x, axes):
    return lax.all_to_all(x, axes, 0, 0, tiled=True)


def gather(x, axes, n):
    return exchange(jnp.broadcast_to(x[None], (n,) + x.shape), axes)


def dot(a, b, dims):
    return lax.dot_general(a, b, (dims, ((), ())), preferred_element_type=F32)


def split3(x):
    hi = x.astype(BF)
    mid = (x - hi.astype(F32)).astype(BF)
    low = (x - hi.astype(F32) - mid.astype(F32)).astype(BF)
    return jnp.stack([hi, mid, low])


def unit_rows(x, weight):
    proj = dot(x, weight, ((1,), (0,)))
    inv = 1.0 / jnp.sqrt(jnp.sum(proj * proj, axis=1, keepdims=True) + 1e-06)
    return (proj * inv).astype(BF), inv


def whole(*s):
    return pl.BlockSpec(s, lambda i: (0,) * len(s))


def first(n, c):
    return pl.BlockSpec((n, c), lambda i: (jnp.minimum(i, HALF // n - 1), 0))


def second(n, c):
    return pl.BlockSpec((n, c), lambda i: (jnp.maximum(i - HALF // n, 0), 0))


def join_kernel(two_ref, a_ref, b_ref, c_ref, after_ref, out_ref):
    n = two_ref.shape[0]
    for k, ref in enumerate((two_ref, a_ref, b_ref, c_ref)):
        out_ref[k * n:(k + 1) * n, :] = ref[...]


def join(two, a, b, c, after):
    n = two.shape[0]
    return pl.pallas_call(
        join_kernel,
        in_specs=[pl.BlockSpec(memory_space=pltpu.VMEM)] * 4 + [pl.BlockSpec(memory_space=pl.ANY)],
        out_specs=pl.BlockSpec(memory_space=pltpu.VMEM),
        out_shape=jax.ShapeDtypeStruct((4 * n, D), BF),
        compiler_params=pltpu.CompilerParams(vmem_limit_bytes=8 << 20),
        cost_estimate=pl.CostEstimate(flops=0, bytes_accessed=16 * n * D, transcendentals=0),
        name="join",
    )(two, a, b, c, after)


def score_step(base, order_ref, x_ref, w_ref, ei_ref, logc_ref, ids_ref, tgt_ref, eq_ref, inv_ref, stat_ref):
    eq, inv_ref[...] = unit_rows(x_ref[...], w_ref[...])
    eq_ref[...] = eq
    power = dot(ei_ref[...], eq, ((1,), (1,))) * (100.0 * LOG2E) - logc_ref[...] * LOG2E
    top = jnp.max(power, axis=0, keepdims=True)
    total = jnp.sum(jnp.exp2(power - top), axis=0, keepdims=True)
    lse = top * (1.0 / LOG2E) + jnp.log(total)
    hit = ids_ref[...] == tgt_ref[...]
    pos = jnp.sum(jnp.where(hit, power, 0.0), axis=0, keepdims=True) * (1.0 / LOG2E)
    for k in range(CH // 128):
        row = order_ref[base + pl.program_id(0) * (CH // 128) + k]
        part = slice(k * 128, (k + 1) * 128)
        stat_ref[pl.ds(row, 1), :] = lse[:, part]
        stat_ref[16:17, :] = stat_ref[16:17, :] + pos[:, part]


def first_kernel(order_ref, x_ref, w_ref, near_ref, far_ref, logc_ref, ids_ref, tgt_ref,
                 eq_ref, inv_ref, ei_ref, invi_ref, stat_ref):
    @pl.when(pl.program_id(0) == 0)
    def _():
        for k, ref in enumerate((near_ref, far_ref)):
            part = slice(k * (IB // 2), (k + 1) * (IB // 2))
            ei_ref[part, :], invi_ref[part, :] = unit_rows(ref[...], w_ref[...])
        stat_ref[...] = jnp.zeros_like(stat_ref)

    score_step(0, order_ref, x_ref, w_ref, ei_ref, logc_ref, ids_ref, tgt_ref, eq_ref, inv_ref, stat_ref)


def second_kernel(order_ref, x_ref, w_ref, ei_ref, logc_ref, ids_ref, tgt_ref, before_ref,
                  eq_ref, inv_ref, stat_ref):
    @pl.when(pl.program_id(0) == 0)
    def _():
        stat_ref[...] = before_ref[...]

    score_step(8, order_ref, x_ref, w_ref, ei_ref, logc_ref, ids_ref, tgt_ref, eq_ref, inv_ref, stat_ref)


def score_call(kernel, base, items, item_specs, item_shapes, order, x, weight, side, targets, tail, name):
    steps = HALF // CH
    return pl.pallas_call(
        kernel,
        grid=(steps,),
        in_specs=[
            pl.BlockSpec(memory_space=pltpu.SMEM),
            pl.BlockSpec((CH, D), lambda i: (i, 0)),
            whole(D, D),
            *[whole(*x.shape) for x in items],
            whole(IB, 1),
            whole(IB, 1),
            pl.BlockSpec((1, CH), lambda i: (0, i + base * steps)),
        ]
        + [whole(24, 128)] * len(tail),
        out_specs=[
            pl.BlockSpec((CH, D), lambda i: (i, 0)),
            pl.BlockSpec((CH, 1), lambda i: (i, 0)),
            *item_specs,
            whole(24, 128),
        ],
        out_shape=[
            jax.ShapeDtypeStruct((HALF, D), BF),
            jax.ShapeDtypeStruct((HALF, 1), F32),
            *item_shapes,
            jax.ShapeDtypeStruct((24, 128), F32),
        ],
        compiler_params=pltpu.CompilerParams(vmem_limit_bytes=24 << 20),
        cost_estimate=pl.CostEstimate(
            flops=2 * HALF * D * (D + IB), bytes_accessed=6 << 20, transcendentals=IB * HALF
        ),
        name=name,
    )(order, x, weight, *items, *side, targets, *tail)


def grad_kernel(core_ref, order_ref, parts_ref, eqa_ref, eqb_ref, inva_ref, invb_ref, xqa_ref, xqb_ref,
                ei_ref, invi_ref, near_ref, far_ref, logc_ref, ids_ref, tgt_ref,
                send_ref, keep_ref, loss_ref, lse_ref, di_ref, acc_ref):
    i = pl.program_id(0)
    core = core_ref[0]

    @pl.when(i == 0)
    def _():
        vals = [parts_ref[d, :16, :] for d in range(16)]
        top = functools.reduce(jnp.maximum, vals)
        lse = top + jnp.log(sum(jnp.exp(v - top) for v in vals))
        lse_ref[...] = lse
        pos = sum(parts_ref[d, 16:17, :] for d in range(16))
        total = jnp.sum(jnp.sum(lse, axis=0, keepdims=True) - pos, axis=1, keepdims=True)
        loss_ref[...] = jnp.broadcast_to(total, (8, 128))
        di_ref[...] = jnp.zeros_like(di_ref)
        acc_ref[...] = jnp.zeros_like(acc_ref)

    def run(eq_ref, inv_ref, xq_ref):
        eq = eq_ref[...]
        rows = [order_ref[i * (CG // 128) + k] for k in range(CG // 128)]
        lse = jnp.concatenate([lse_ref[pl.ds(r, 1), :] for r in rows], axis=1)
        power = dot(ei_ref[...], eq, ((1,), (1,))) * (100.0 * LOG2E) - logc_ref[...] * LOG2E
        prob = jnp.exp2(power - (lse * LOG2E - LOG2_NORM))
        grad = jnp.where(ids_ref[...] == tgt_ref[...], prob - INV_NORM, prob).astype(BF)
        di_ref[...] += dot(grad, eq, ((1,), (0,)))
        dq = dot(grad, ei_ref[...], ((0,), (0,)))
        eq = eq.astype(F32)
        inner = jnp.sum(eq * dq, axis=1, keepdims=True)
        dz = ((dq - eq * inner) * (100.0 * inv_ref[...])).astype(BF)
        acc_ref[...] += dot(xq_ref[...], dz, ((0,), (0,)))

    @pl.when(i < HALF // CG)
    def _():
        run(eqa_ref, inva_ref, xqa_ref)

    @pl.when(i >= HALF // CG)
    def _():
        run(eqb_ref, invb_ref, xqb_ref)

    @pl.when(i == QB // CG - 1)
    def _():
        di = 100.0 * di_ref[...]
        ei = ei_ref[...].astype(F32)
        inner = jnp.sum(ei * di, axis=1, keepdims=True)
        dz = ((di - ei * inner) * invi_ref[...]).astype(BF)
        for k, ref in enumerate((near_ref, far_ref)):
            acc_ref[...] += dot(ref[...], dz[k * (IB // 2):(k + 1) * (IB // 2)], ((0,), (0,)))
        mine = pl.ds(pl.multiple_of(core * (D // 2), D // 2), D // 2)
        theirs = pl.ds(pl.multiple_of((1 - core) * (D // 2), D // 2), D // 2)
        keep_ref[...] = acc_ref[mine, :].astype(BF)
        send_ref[...] = acc_ref[theirs, :].astype(BF)


def grads(core, order, parts, eqa, eqb, inva, invb, xqa, xqb, ei, invi, near, far, logc, ids, targets):
    return pl.pallas_call(
        grad_kernel,
        grid=(QB // CG,),
        in_specs=[
            pl.BlockSpec(memory_space=pltpu.SMEM),
            pl.BlockSpec(memory_space=pltpu.SMEM),
            whole(16, 24, 128),
            first(CG, D),
            second(CG, D),
            first(CG, 1),
            second(CG, 1),
            first(CG, D),
            second(CG, D),
            whole(IB, D),
            whole(IB, 1),
            whole(IB // 2, D),
            whole(IB // 2, D),
            whole(IB, 1),
            whole(IB, 1),
            pl.BlockSpec((1, CG), lambda i: (0, i)),
        ],
        out_specs=[whole(D // 2, D), whole(D // 2, D), whole(8, 128)],
        out_shape=[
            jax.ShapeDtypeStruct((D // 2, D), BF),
            jax.ShapeDtypeStruct((D // 2, D), BF),
            jax.ShapeDtypeStruct((8, 128), F32),
        ],
        scratch_shapes=[
            pltpu.VMEM((16, 128), F32),
            pltpu.VMEM((IB, D), F32),
            pltpu.VMEM((D, D), F32),
        ],
        compiler_params=pltpu.CompilerParams(vmem_limit_bytes=32 << 20),
        cost_estimate=pl.CostEstimate(
            flops=2 * IB * D * 3 * QB + 2 * D * D * (QB + IB), bytes_accessed=9 << 20, transcendentals=IB * QB
        ),
        name="grads",
    )(core, order, parts, eqa, eqb, inva, invb, xqa, xqb, ei, invi, near, far, logc, ids, targets)


def body(xq_own, xi_own, weight, counts, positives):
    core, y, xh = lax.axis_index("c"), lax.axis_index("y"), lax.axis_index("xh")
    xl = lax.axis_index("xl")
    near = gather(xi_own, "z", 16).reshape(IB // 2, D)
    far = swap(near, "xl")
    two = jnp.concatenate([xq_own, swap(xq_own, "xh")])
    xqa = join(two, turn(two, 1), turn(two, 3), turn(two, 2), far)
    xqb = swap(xqa, "c")

    q = lax.iota(jnp.int32, 16)
    step = (q // 2) % 4
    from_y = (y + jnp.where(step == 1, 3, jnp.where(step == 2, 1, jnp.where(step == 3, 2, 0)))) % 4
    order = from_y * 4 + (xh ^ (q % 2)) * 2 + (core ^ (q // 8))
    picks = order[:, None, None] == q[None, :, None]
    targets = jnp.sum(jnp.where(picks, positives.reshape(1, 16, 128), 0), axis=1).reshape(1, QB)
    block = (y * 2 + xh) * 2 + core
    weight, near = pltpu.with_memory_space_constraint(weight, pltpu.HBM), pltpu.with_memory_space_constraint(near, pltpu.HBM)
    at = lax.iota(jnp.int32, IB)
    ids = ((at // 16) % 16 * 2 + (xl ^ (at // 256))) * 16 + at % 16
    logs = jnp.log(counts.astype(F32))
    logc = jnp.sum(jnp.where(ids[:, None] == at[None, :], logs[None, :], 0.0), axis=1, keepdims=True)
    ids = (block * IB + ids)[:, None]

    eqa, inva, ei, invi, stat = score_call(
        first_kernel,
        0,
        (near, far),
        [whole(IB, D), whole(IB, 1)],
        [jax.ShapeDtypeStruct((IB, D), BF), jax.ShapeDtypeStruct((IB, 1), F32)],
        order, xqa, weight, (logc, ids), targets, (), "score_first",
    )
    eqb, invb, stat = score_call(
        second_kernel, 1, (ei,), [], [], order, xqb, weight, (logc, ids), targets, (stat,), "score_second"
    )
    parts = gather(stat, POOL, 16)
    send, keep, loss = grads(
        core.reshape(1), order, parts, eqa, eqb, inva, invb, xqa, xqb, ei, invi, near, far, logc, ids, targets
    )

    loss = (loss + swap(loss, "xl"))[0, 0] / ROWS
    s = (keep.astype(F32) + swap(send, "c").astype(F32)).astype(BF)
    s = jnp.sum(exchange(s.reshape(16, 24, D), YXX).astype(F32), axis=0).astype(BF)
    tail = jnp.zeros((7, 128), BF).at[0, :3].set(split3(loss))
    tail = jnp.broadcast_to(tail[None], (16, 7, 128))
    s = exchange(jnp.concatenate([s.reshape(16, 9, 128), tail], axis=1), "z")
    s = jnp.sum(s.astype(F32), axis=0)
    mean_loss = jnp.sum(s[9, :3])
    s = gather(s.astype(BF), "z", 16)[:, :9]
    s = gather(s.reshape(24, D), YXX, 16).reshape(D // 2, D)
    other = swap(s, "c")
    first, second = jnp.where(core == 0, s, other), jnp.where(core == 0, other, s)
    return mean_loss, jnp.concatenate([first, second]).astype(F32)


def solution(mesh):
    fine = Mesh(mesh.devices.reshape(4, 2, 2, 16, 2), ("y", "xh", "c", "z", "xl"))
    batch = ("z", "xl")
    return jax.shard_map(
        body,
        mesh=fine,
        in_specs=(P(batch + POOL, None), P(POOL + batch, None), P(), P(POOL), P(batch)),
        out_specs=(P(), P()),
        check_vma=False,
    )
```
